256 devices in a mesh: ctx: 32 (over z, x_hi, core), head: 8 (over x_lo, y).
Axes of the slice: x: 4 (x_hi: 2, x_lo: 2; x = x_hi * 2 + x_lo), y: 4, z: 8, core: 2. Of those that a mesh axis runs over, the one named last changes fastest.
Arguments:
- queries: bfloat16 [32768, 4096], P('ctx', 'head'), may hold values from -6 to 6
- token_keys: bfloat16 [32768, 4096], P('ctx', 'head'), may hold values from -6 to 6
- values: bfloat16 [32768, 4096], P('ctx', 'head'), may hold values from -6 to 6
- step_rates: float32 [8, 32768], P('head', 'ctx'), may hold values from 0.01 to 0.3
- window_blocks: int32 [8, 64], P('head', 'ctx'), may hold values from 0 to 2, as said below
- fast_gate: bfloat16 [8, 512, 512], P('head'), may hold values from -0.25 to 0.25
- fast_up: bfloat16 [8, 512, 512], P('head'), may hold values from -0.25 to 0.25
- fast_down: bfloat16 [8, 512, 512], P('head'), may hold values from -0.25 to 0.25
- norm_gain: float32 [8, 512], P('head'), may hold values from 0.1 to 1.9
- out_weight: bfloat16 [4096, 5120], P(None, 'head'), may hold values from -0.09375 to 0.09375
Outputs:
- layer_out: bfloat16 [32768, 5120], P('ctx', 'head')
The draws below stay inside these ranges and needn't reach their ends.
Inputs may be any that keep to these rules, and one draw needn't show every extreme that they name: `window_blocks`: how many earlier blocks of 512 tokens each query block of each head may see.
All inputs are finite; a program needn't handle non-finite values.
Results may differ from the reference program's by a relative error of at most 0.029.
Values may be sent and summed in bfloat16 or wider, within the bound.
A program may use at most 64 MiB of HBM per device.

```python
import math
import jax
import jax.numpy as jnp
from jax import lax

D = 5120
H = 8
HD = 512
FH = 512
BL = 512
WIN = 2
TOKENS = 32768
NBLK = 64


def paired_draw(key):
    full_shape = (TOKENS, H * HD)
    query_draw = jnp.clip(jax.random.normal(jax.random.fold_in(key, 11), full_shape, jnp.float32), -6.0, 6.0)
    key_draw = jnp.clip(jax.random.normal(jax.random.fold_in(key, 12), full_shape, jnp.float32), -6.0, 6.0)
    return (query_draw, key_draw)


def draw_queries(key, part):
    return paired_draw(key)[0].astype(jnp.bfloat16)


def draw_token_keys(key, part):
    return paired_draw(key)[1].astype(jnp.bfloat16)


def draw_window_blocks(key, part):
    base_draw = jax.random.randint(jax.random.fold_in(key, 21), (H, NBLK), 0, WIN + 1)
    head_top = jax.random.randint(jax.random.fold_in(key, 22), (), 0, H)
    block_top = jax.random.randint(jax.random.fold_in(key, 23), (), 0, NBLK)
    head_low = jax.random.randint(jax.random.fold_in(key, 24), (), 0, H)
    block_low = (block_top + 1 + jax.random.randint(jax.random.fold_in(key, 25), (), 0, NBLK - 1)) % NBLK
    base_draw = base_draw.at[head_top, block_top].set(WIN)
    base_draw = base_draw.at[head_low, block_low].set(0)
    return base_draw.astype(jnp.int32)


def levels(rng, dims, shards, least, high):
    gain = 1.0
    for position, parts in shards:
        draws = jax.random.uniform(jax.random.fold_in(jax.random.fold_in(rng, 6), position), (parts,), jnp.float32, least / len(shards), high / len(shards))
        gain = gain * jnp.repeat(jnp.exp(draws), dims[position] // parts).reshape((-1,) + (1,) * (len(dims) - 1 - position))
    return gain


def normal_values(own_key, shape, width, limit, cuts=(), held_as=jnp.bfloat16):
    drawn = width * jax.random.normal(own_key, shape, jnp.float32)
    if cuts:
        drawn = drawn * levels(own_key, shape, cuts, -0.22, 0.18)
    return jnp.clip(drawn, -limit, limit).astype(held_as)


def setup_inputs(seed: int = 0) -> dict:
    keys = jax.random.split(jax.random.key(seed), 11)
    queries = draw_queries(jax.random.fold_in(keys[10], 71), 0)
    token_keys = draw_token_keys(jax.random.fold_in(keys[10], 71), 0)
    values = normal_values(keys[2], (TOKENS, H * HD), 1.0, 6.0, ((0, 32), (1, 8)))
    step_rates = jnp.clip(jnp.exp(math.log(0.3) - 3.4011974 * jax.random.uniform(keys[3], (H, TOKENS), jnp.float32) ** levels(keys[3], (H, TOKENS), ((0, 8), (1, 32)), -0.2, 0.2)), 0.01, 0.3)
    window_blocks = draw_window_blocks(jax.random.fold_in(keys[10], 71), 0)
    fast_gate = normal_values(keys[5], (H, HD, FH), HD ** -0.5, 0.25, ((0, 8),))
    fast_up = normal_values(keys[6], (H, HD, FH), HD ** -0.5, 0.25, ((0, 8),))
    fast_down = normal_values(keys[7], (H, FH, HD), FH ** -0.5, 0.25, ((0, 8),))
    norm_gain = jnp.clip(1.0 + 0.18 * jax.random.normal(keys[8], (H, HD), jnp.float32), 0.1, 1.9)
    out_weight = normal_values(keys[9], (H * HD, D), (H * HD) ** -0.5, 0.09375, ((1, 8),))
    return dict(queries=queries, token_keys=token_keys, values=values, step_rates=step_rates, window_blocks=window_blocks, fast_gate=fast_gate, fast_up=fast_up, fast_down=fast_down, norm_gain=norm_gain, out_weight=out_weight)


grad_limit = 24.0
epsilon = 1e-06

def silu_pair(inputs):
    sigmoid = jax.nn.sigmoid(inputs)
    return (inputs * sigmoid, sigmoid * (1.0 + inputs * (1.0 - sigmoid)))

def renewed(weight, gradient, factor):
    start_weight = weight.astype(jnp.float32)
    moved = start_weight - factor * gradient
    before = jnp.sqrt(lax.optimization_barrier(jnp.sum(start_weight * start_weight, axis=-2, keepdims=True)) + epsilon)
    after = jnp.sqrt(lax.optimization_barrier(jnp.sum(moved * moved, axis=-2, keepdims=True)) + epsilon)
    return (moved * (before / after)).astype(jnp.bfloat16)

def window_attend(query_head, key_head, value_head, window_head):
    halo_rows = WIN * BL
    padded_keys = jnp.pad(key_head, ((halo_rows, 0), (0, 0)))
    padded_values = jnp.pad(value_head, ((halo_rows, 0), (0, 0)))
    score_scale = HD ** (-0.5)

    def one_block(block_id):
        query_block = lax.dynamic_slice_in_dim(query_head, block_id * BL, BL, 0)
        key_block = lax.dynamic_slice_in_dim(padded_keys, block_id * BL, (WIN + 1) * BL, 0)
        value_block = lax.dynamic_slice_in_dim(padded_values, block_id * BL, (WIN + 1) * BL, 0)
        scores = jnp.dot(query_block, key_block.T, preferred_element_type=jnp.float32) * score_scale
        query_pos = block_id * BL + jnp.arange(BL, dtype=jnp.int32)
        key_pos = block_id * BL - halo_rows + jnp.arange((WIN + 1) * BL, dtype=jnp.int32)
        reach_blocks = window_head[block_id]
        visible = (key_pos[None, :] <= query_pos[:, None]) & (key_pos[None, :] >= 0) & (key_pos[None, :] // BL >= block_id - reach_blocks)
        scores = jnp.where(visible, scores, -jnp.inf)
        row_top = lax.optimization_barrier(jnp.max(scores, axis=-1, keepdims=True))
        raised = jnp.exp(scores - row_top)
        weights_bf = (raised / lax.optimization_barrier(jnp.sum(raised, axis=-1, keepdims=True))).astype(jnp.bfloat16)
        return jnp.dot(weights_bf, value_block, preferred_element_type=jnp.float32)
    attended = lax.map(one_block, jnp.arange(NBLK, dtype=jnp.int32))
    return attended.reshape(TOKENS, HD)

def fast_head(operands):
    query_head, key_head, value_head, rate_head, gate_head, up_head, down_head, gain_head, window_head = operands
    gate_pre = jnp.dot(key_head, gate_head, preferred_element_type=jnp.float32)
    up_pre = jnp.dot(key_head, up_head, preferred_element_type=jnp.float32)
    silu_val, silu_slope = silu_pair(gate_pre)
    hidden_act = (silu_val * up_pre).astype(jnp.bfloat16)
    target = (-rate_head[:, None] * value_head.astype(jnp.float32)).astype(jnp.bfloat16)
    grad_down = jnp.dot(hidden_act.T, target, preferred_element_type=jnp.float32)
    back_act = jnp.dot(target, down_head.T, preferred_element_type=jnp.float32)
    back_gate = (back_act * up_pre * silu_slope).astype(jnp.bfloat16)
    back_up = (back_act * silu_val).astype(jnp.bfloat16)
    grad_gate = jnp.dot(key_head.T, back_gate, preferred_element_type=jnp.float32)
    grad_up = jnp.dot(key_head.T, back_up, preferred_element_type=jnp.float32)
    squared = jnp.sum(grad_gate * grad_gate) + jnp.sum(grad_up * grad_up) + jnp.sum(grad_down * grad_down)
    gnorm = jnp.sqrt(squared + epsilon)
    factor = jnp.minimum(1.0, grad_limit / gnorm)
    new_gate = renewed(gate_head, grad_gate, factor)
    new_up = renewed(up_head, grad_up, factor)
    new_down = renewed(down_head, grad_down, factor)
    query_gate = jnp.dot(query_head, new_gate, preferred_element_type=jnp.float32)
    query_up = jnp.dot(query_head, new_up, preferred_element_type=jnp.float32)
    query_silu, unused_slope = silu_pair(query_gate)
    read_act = (query_silu * query_up).astype(jnp.bfloat16)
    fast_out = jnp.dot(read_act, new_down, preferred_element_type=jnp.float32)
    normed = fast_out * lax.rsqrt(lax.optimization_barrier(jnp.mean(fast_out * fast_out, axis=-1, keepdims=True)) + epsilon) * gain_head[None, :]
    attended = window_attend(query_head, key_head, value_head, window_head)
    return (normed + attended).astype(jnp.bfloat16)

def reference(queries, token_keys, values, step_rates, window_blocks, fast_gate, fast_up, fast_down, norm_gain, out_weight):
    query_heads = queries.reshape(TOKENS, H, HD).transpose(1, 0, 2)
    key_heads = token_keys.reshape(TOKENS, H, HD).transpose(1, 0, 2)
    value_heads = values.reshape(TOKENS, H, HD).transpose(1, 0, 2)
    stacked = lax.map(fast_head, (query_heads, key_heads, value_heads, step_rates, fast_gate, fast_up, fast_down, norm_gain, window_blocks))
    readout = stacked.transpose(1, 0, 2).reshape(TOKENS, H * HD)
    return jnp.dot(readout, out_weight, preferred_element_type=jnp.float32).astype(jnp.bfloat16)
```

```python
import jax
import jax.numpy as jnp
from jax import lax
from jax.sharding import PartitionSpec as P
from jax.experimental import pallas as pl
from jax.experimental.pallas import tpu as pltpu

MESH = pl.DeviceIdType.MESH
F32 = jnp.float32
BF16 = jnp.bfloat16

TOK = 1024
HD = 512
BL = 512
HALO = 1024
NZ = 8
NY = 4
HEADS = 8
COLS = 640
HALF = 256
QUART = 128
SHARD = 16
TT = 256
NT = TOK // TT
GT = 128
NG = TOK // GT
GRAD_LIMIT = 24.0
EPS = 1e-6
MASKED = -1e30


def sigmoid(x):
    return 0.5 * jnp.tanh(0.5 * x) + 0.5


def dot(a, b):
    return jnp.dot(a, b, preferred_element_type=F32)


def dot_nt(a, b):
    return lax.dot_general(a, b, (((1,), (1,)), ((), ())), preferred_element_type=F32)


def dot_tn(a, b):
    return lax.dot_general(a, b, (((0,), (0,)), ((), ())), preferred_element_type=F32)


def tile_kind(t):
    return "A" if t % 2 == 0 else "B"


def body(
    q_ref, k_ref, v_ref, rate_ref, win_ref, w1_ref, w3_ref, w2_ref, gain_ref, wo_ref,
    out_ref,
    q, k, v, hk, hv, w1, w3, w2, wo, rate, gain,
    hid, tgt, bg, bu,
    sib_send, sib_recv, own, xh_send, xh_recv, z_send, z_recv, gfull,
    n1, n3, n2, m_run, l_run, acc, gat, outv,
    load_sem, out_sem, halo_ss, halo_rs, sib_ss, sib_rs, xh_ss, xh_rs, z_ss, z_rs,
    ag_ss, ag_rs, xg_ss, xg_rs, sg_ss, sg_rs, gy_ss, gx_ss, g_rs,
):
    ctx = lax.axis_index("ctx")
    head = lax.axis_index("head")
    z = ctx // 4
    xh = (ctx // 2) % 2
    core = ctx % 2
    xl = head // 4
    y = head % 4

    def at_ctx(zz, xx, cc):
        return (zz * 4 + xx * 2 + cc, head)

    def at_head(xx, yy):
        return (ctx, xx * 4 + yy)

    sib = at_ctx(z, xh, 1 - core)
    xhp = at_ctx(z, 1 - xh, core)
    zpeer = [None] + [at_ctx((z + d) % NZ, xh, core) for d in range(1, NZ)]
    nxt = ((ctx + 1) % 32, head)
    prv = ((ctx + 31) % 32, head)
    xp = at_head(1 - xl, y)
    yp = at_head(xl, (y + 1) % NY)
    ym = at_head(xl, (y + 3) % NY)

    bar = pltpu.get_barrier_semaphore()
    partners = [sib, xhp] + zpeer[1:] + [xp, yp, ym, prv]
    for p in partners:
        pl.semaphore_signal(bar, inc=1, device_id=p, device_id_type=MESH)

    loads = []
    for i, (src, dst) in enumerate(
        ((k_ref, k), (w1_ref, w1), (w3_ref, w3), (w2_ref, w2), (rate_ref, rate), (v_ref, v),
         (q_ref, q), (gain_ref, gain), (wo_ref, wo))
    ):
        c = pltpu.make_async_copy(src, dst, load_sem.at[i])
        c.start()
        loads.append(c)

    pl.semaphore_wait(bar, len(partners))

    sends = []

    def send(src, dst, ss, rs, dev):
        c = pltpu.make_async_remote_copy(
            src_ref=src, dst_ref=dst, send_sem=ss, recv_sem=rs, device_id=dev, device_id_type=MESH
        )
        c.start()
        sends.append(c)
        return c

    def arrived(dst, rs):
        pltpu.make_async_remote_copy(
            src_ref=dst, dst_ref=dst, send_sem=rs, recv_sem=rs, device_id=sib, device_id_type=MESH
        ).wait_recv()

    send(k_ref, hk, halo_ss.at[0], halo_rs.at[0], nxt)
    send(v_ref, hv, halo_ss.at[1], halo_rs.at[1], nxt)

    for c in loads[:6]:
        c.wait()

    def grad_tile(t, carry):
        r = pl.ds(pl.multiple_of(t * TT, TT), TT)
        kt = k[r, :]
        gp = dot(kt, w1[0])
        up = dot(kt, w3[0])
        s = sigmoid(gp)
        sv = gp * s
        hid[r, :] = (sv * up).astype(BF16)
        row = rate[:, r]
        eye = lax.broadcasted_iota(jnp.int32, (TT, TT), 0) == lax.broadcasted_iota(
            jnp.int32, (TT, TT), 1
        )
        col = jnp.sum(jnp.where(eye, row, 0.0), axis=1, keepdims=True)
        tg = (-col * v[r, :].astype(F32)).astype(BF16)
        tgt[r, :] = tg
        ba = dot_nt(tg, w2[0])
        bg[r, :] = (ba * up * (s * (1.0 + gp * (1.0 - s)))).astype(BF16)
        bu[r, :] = (ba * sv).astype(BF16)
        return carry

    lax.fori_loop(0, NT, grad_tile, 0)

    theirs = pl.ds(pl.multiple_of((1 - core) * HALF, HALF), HALF)
    mine = pl.ds(pl.multiple_of(core * HALF, HALF), HALF)
    pairs = ((hid, tgt), (k, bg), (k, bu))
    for m, (a, b) in enumerate(pairs):
        sib_send[m] = dot_tn(a[:, theirs], b[...]).astype(BF16)
        send(sib_send.at[m], sib_recv.at[m], sib_ss.at[m], sib_rs.at[m], sib)
    for m, (a, b) in enumerate(pairs):
        own[m] = dot_tn(a[:, mine], b[...])

    x_theirs = pl.ds(pl.multiple_of((1 - xh) * QUART, QUART), QUART)
    x_mine = pl.ds(pl.multiple_of(xh * QUART, QUART), QUART)
    for m in range(3):
        arrived(sib_recv.at[m], sib_rs.at[m])
        xh_send[m] = (own[m, x_theirs, :] + sib_recv[m, x_theirs, :].astype(F32)).astype(BF16)
        send(xh_send.at[m], xh_recv.at[m], xh_ss.at[m], xh_rs.at[m], xhp)
        own[m, x_mine, :] = own[m, x_mine, :] + sib_recv[m, x_mine, :].astype(F32)

    for c in loads[6:8]:
        c.wait()
    scale = HD ** -0.5
    reach = [win_ref[0, 0], win_ref[0, 1]]

    def own_tile(t):
        r = pl.ds(t * TT, TT)
        blk = t // 2
        width = (t + 1) * TT
        s = dot_nt(q[r, :], k[pl.ds(0, width), :]) * scale
        qpos = lax.broadcasted_iota(jnp.int32, (TT, width), 0) + t * TT
        kpos = lax.broadcasted_iota(jnp.int32, (TT, width), 1)
        s = jnp.where(kpos <= qpos, s, MASKED)
        if blk == 1:
            far = jnp.where(reach[1] >= 1, 0.0, MASKED)
            s = s + jnp.where(kpos < BL, far, 0.0)
        top = jnp.max(s, axis=1, keepdims=True)
        p = jnp.exp(s - top)
        m_run[r, :] = top
        l_run[r, :] = jnp.sum(p, axis=1, keepdims=True)
        acc[r, :] = dot(p.astype(BF16), v[pl.ds(0, width), :])

    first = ctx == 0

    def halo_tile(t):
        r = pl.ds(t * TT, TT)
        blk = t // 2
        if blk == 0:
            lo, width = 0, HALO
        else:
            lo, width = BL, BL
        s = dot_nt(q[r, :], hk[pl.ds(lo, width), :]) * scale
        near = jnp.where(jnp.logical_or(reach[blk] < (1 if blk == 0 else 2), first), MASKED, 0.0)
        if blk == 0:
            far = jnp.where(jnp.logical_or(reach[blk] < 2, first), MASKED, 0.0)
            kpos = lax.broadcasted_iota(jnp.int32, (TT, width), 1)
            s = s + jnp.where(kpos < BL, far, near)
        else:
            s = s + near
        old = m_run[r, :]
        top = jnp.maximum(old, jnp.max(s, axis=1, keepdims=True))
        p = jnp.exp(s - top)
        keep = jnp.exp(old - top)
        total = l_run[r, :] * keep + jnp.sum(p, axis=1, keepdims=True)
        o = acc[r, :] * keep + dot(p.astype(BF16), hv[pl.ds(lo, width), :])
        acc[r, :] = o / total

    own_tile(0)
    own_tile(1)

    for m in range(3):
        arrived(xh_recv.at[m], xh_rs.at[m])
        red = own[m, x_mine, :] + xh_recv[m].astype(F32)
        own[m, x_mine, :] = red
        z_send[m] = red.astype(BF16)
        for d in range(1, NZ):
            dest = (z + d) % NZ
            send(
                z_send.at[m, pl.ds(pl.multiple_of(dest * SHARD, SHARD), SHARD)],
                z_recv.at[m, d - 1], z_ss.at[m, d - 1], z_rs.at[m, d - 1], zpeer[d],
            )

    own_tile(2)
    own_tile(3)

    base = core * HALF + xh * QUART
    z_mine = pl.ds(pl.multiple_of(xh * QUART + z * SHARD, SHARD), SHARD)
    for m in range(3):
        total = own[m, z_mine, :]
        for d in range(1, NZ):
            arrived(z_recv.at[m, d - 1], z_rs.at[m, d - 1])
            total = total + z_recv[m, d - 1].astype(F32)
        rows = pl.ds(pl.multiple_of(base + z * SHARD, SHARD), SHARD)
        gfull[m, rows, :] = total.astype(BF16)
        for d in range(1, NZ):
            send(gfull.at[m, rows], gfull.at[m, rows], ag_ss.at[m, d - 1], ag_rs.at[m, d - 1], zpeer[d])

    arrived(hk, halo_rs.at[0])
    arrived(hv, halo_rs.at[1])
    halo_tile(0)
    halo_tile(1)

    blk_z = pl.ds(pl.multiple_of(base, QUART), QUART)
    blk_x = pl.ds(pl.multiple_of(core * HALF + (1 - xh) * QUART, QUART), QUART)
    for m in range(3):
        for d in range(1, NZ):
            src = (z + NZ - d) % NZ
            rows = pl.ds(pl.multiple_of(base + src * SHARD, SHARD), SHARD)
            arrived(gfull.at[m, rows], ag_rs.at[m, d - 1])
        send(gfull.at[m, blk_z], gfull.at[m, blk_z], xg_ss.at[m], xg_rs.at[m], xhp)
        send(gfull.at[m, blk_z], gfull.at[m, blk_z], sg_ss.at[m, 0], sg_rs.at[m, 0], sib)

    halo_tile(2)
    halo_tile(3)

    for m in range(3):
        arrived(gfull.at[m, blk_x], xg_rs.at[m])
        send(gfull.at[m, blk_x], gfull.at[m, blk_x], sg_ss.at[m, 1], sg_rs.at[m, 1], sib)
    squares = jnp.zeros((1, HD), F32)
    for m in range(3):
        for j in range(2):
            half = pl.ds(
                pl.multiple_of((1 - core) * HALF + (xh if j == 0 else 1 - xh) * QUART, QUART), QUART
            )
            arrived(gfull.at[m, half], sg_rs.at[m, j])
        g = gfull[m].astype(F32)
        squares = squares + jnp.sum(g * g, axis=0, keepdims=True)

    gnorm = jnp.sqrt(jnp.sum(squares, axis=1, keepdims=True) + EPS)
    factor = jnp.minimum(1.0, GRAD_LIMIT / gnorm)
    for m, (old, new) in enumerate(((w2, n2), (w1, n1), (w3, n3))):
        w = old[0].astype(F32)
        u = w - factor * gfull[m].astype(F32)
        before = jnp.sqrt(jnp.sum(w * w, axis=0, keepdims=True) + EPS)
        after = jnp.sqrt(jnp.sum(u * u, axis=0, keepdims=True) + EPS)
        new[...] = (u * (before / after)).astype(BF16)

    def slot(h, t):
        return gat.at[h, pl.ds(t * GT, GT)]

    def pass_on(h, t, way):
        s = slot(h, t)
        if way == "x":
            send(s, s, gx_ss.at[t, h], g_rs.at[t, h], xp)
        elif way == "+":
            send(s, s, gy_ss.at[0, t, h], g_rs.at[t, h], yp)
        else:
            send(s, s, gy_ss.at[1, t, h], g_rs.at[t, h], ym)

    cols = [xl * 4 + (y + j) % NY for j in range(NY)]
    crss = [(1 - xl) * 4 + (y + j) % NY for j in range(NY)]

    for t in range(NT):
        r = pl.ds(t * TT, TT)
        qt = q[r, :]
        g = dot(qt, n1[...])
        u = dot(qt, n3[...])
        a = (g * sigmoid(g) * u).astype(BF16)
        f = dot(a, n2[...])
        ms = jnp.mean(f * f, axis=1, keepdims=True)
        nrm = f * lax.rsqrt(ms + EPS) * gain[...]
        gat[cols[0], r, :] = (nrm + acc[r, :]).astype(BF16)
        for tt in range(t * TT // GT, (t + 1) * TT // GT):
            for way in ("x", "+", "-"):
                pass_on(cols[0], tt, way)

    loads[8].wait()

    def got(h, t):
        arrived(slot(h, t), g_rs.at[t, h])

    for t in range(NG):
        if tile_kind(t) == "A":
            got(crss[0], t)
            pass_on(crss[0], t, "+")
            pass_on(crss[0], t, "-")
            got(cols[3], t)
            pass_on(cols[3], t, "+")
            got(cols[1], t)
            got(crss[1], t)
            pass_on(crss[1], t, "-")
            got(crss[3], t)
            got(cols[2], t)
            got(crss[2], t)
        else:
            plus = (t // 2) % 2 == 0
            got(cols[3], t)
            if plus:
                pass_on(cols[3], t, "+")
            pass_on(cols[3], t, "x")
            got(cols[1], t)
            if not plus:
                pass_on(cols[1], t, "-")
            pass_on(cols[1], t, "x")
            got(cols[2], t)
            pass_on(cols[2], t, "x")
            for j in (0, 3, 1, 2):
                got(crss[j], t)
        if (t + 1) * GT % TT == 0:
            r = pl.ds((t + 1) * GT - TT, TT)
            o = dot(gat[0, r, :], wo[pl.ds(0, HD), :])
            for h in range(1, HEADS):
                o = o + dot(gat[h, r, :], wo[pl.ds(h * HD, HD), :])
            outv[r, :] = o.astype(BF16)
            i = (t + 1) * GT // TT - 1
            pltpu.make_async_copy(outv.at[r], out_ref.at[r], out_sem.at[i]).start()

    for i in range(NT):
        r = pl.ds(i * TT, TT)
        pltpu.make_async_copy(outv.at[r], out_ref.at[r], out_sem.at[i]).wait()
    for c in sends:
        c.wait_send()


def per_device(*args):
    any_spec = pl.BlockSpec(memory_space=pl.ANY)
    in_specs = [any_spec] * 10
    in_specs[4] = pl.BlockSpec(memory_space=pltpu.SMEM)
    V = pltpu.VMEM
    D = pltpu.SemaphoreType.DMA
    scratch = [
        V((TOK, HD), BF16), V((TOK, HD), BF16), V((TOK, HD), BF16),
        V((HALO, HD), BF16), V((HALO, HD), BF16),
        V((1, HD, HD), BF16), V((1, HD, HD), BF16), V((1, HD, HD), BF16),
        V((HEADS * HD, COLS), BF16), V((1, TOK), F32), V((1, HD), F32),
        V((TOK, HD), BF16), V((TOK, HD), BF16), V((TOK, HD), BF16), V((TOK, HD), BF16),
        V((3, HALF, HD), BF16), V((3, HALF, HD), BF16), V((3, HALF, HD), F32),
        V((3, QUART, HD), BF16), V((3, QUART, HD), BF16),
        V((3, QUART, HD), BF16), V((3, NZ - 1, SHARD, HD), BF16), V((3, HD, HD), BF16),
        V((HD, HD), BF16), V((HD, HD), BF16), V((HD, HD), BF16),
        V((TOK, 1), F32), V((TOK, 1), F32), V((TOK, HD), F32),
        V((HEADS, TOK, HD), BF16), V((TOK, COLS), BF16),
        D((9,)), D((NT,)), D((2,)), D((2,)), D((3,)), D((3,)), D((3,)), D((3,)),
        D((3, NZ - 1)), D((3, NZ - 1)), D((3, NZ - 1)), D((3, NZ - 1)),
        D((3,)), D((3,)), D((3, 2)), D((3, 2)),
        D((2, NG, HEADS)), D((NG, HEADS)), D((NG, HEADS)),
    ]
    return pl.pallas_call(
        body,
        out_shape=jax.ShapeDtypeStruct((TOK, COLS), BF16),
        in_specs=in_specs,
        out_specs=any_spec,
        scratch_shapes=scratch,
        compiler_params=pltpu.CompilerParams(
            collective_id=0, has_side_effects=True, vmem_limit_bytes=60 << 20
        ),
        cost_estimate=pl.CostEstimate(flops=13_400_000_000, bytes_accessed=15_000_000, transcendentals=3_000_000),
        name="ttt_layer",
    )(*args)


def solution(mesh):
    placed = (
        P("ctx", "head"),
        P("ctx", "head"),
        P("ctx", "head"),
        P("head", "ctx"),
        P("head", "ctx"),
        P("head", None, None),
        P("head", None, None),
        P("head", None, None),
        P("head", None),
        P(None, "head"),
    )
    return jax.shard_map(
        per_device, mesh=mesh, in_specs=placed, out_specs=P("ctx", "head"), check_vma=False
    )
```

```python
import jax
import jax.numpy as jnp
from jax import lax
from jax.sharding import PartitionSpec as P
from jax.experimental import pallas as pl
from jax.experimental.pallas import tpu as pltpu

MESH = pl.DeviceIdType.MESH
F32 = jnp.float32
BF16 = jnp.bfloat16

TOK = 1024
HD = 512
BL = 512
HALO = 1024
NZ = 8
NY = 4
HEADS = 8
COLS = 640
HALF = 256
SHARD = 32
HOPS = NZ // 2
TT = 256
NT = TOK // TT
GT = 128
NG = TOK // GT
HP = 128
GRAD_LIMIT = 24.0
EPS = 1e-6
MASKED = -1e30


def sigmoid(x):
    return 0.5 * jnp.tanh(0.5 * x) + 0.5


def dot(a, b):
    return jnp.dot(a, b, preferred_element_type=F32)


def dot_nt(a, b):
    return lax.dot_general(a, b, (((1,), (1,)), ((), ())), preferred_element_type=F32)


def dot_tn(a, b):
    return lax.dot_general(a, b, (((0,), (0,)), ((), ())), preferred_element_type=F32)


def far_way(m):
    return m % 2


def tile_kind(t):
    return "A" if t % 2 == 0 else "B"


def body(
    q_ref, k_ref, v_ref, rate_ref, win_ref, w1_ref, w3_ref, w2_ref, gain_ref, wo_ref,
    out_ref,
    q, k, v, hk, hv, w1, w3, w2, wo, rate, gain,
    hid, tgt, bg, bu,
    sib_send, sib_recv, own, rs_send, rs_recv, x_send, x_recv, gfull,
    n1, n3, n2, m_run, l_run, acc, gat, outv,
    load_sem, out_sem, halo_ss, halo_rs, sib_ss, sib_rs, rs_ss, rs_rs, x_ss, x_rs,
    ag_ss, ag_rs, sg_ss, sg_rs, gy_ss, gx_ss, g_rs,
):
    ctx = lax.axis_index("ctx")
    head = lax.axis_index("head")
    z = ctx // 4
    xh = (ctx // 2) % 2
    core = ctx % 2
    xl = head // 4
    y = head % 4

    def at_ctx(zz, xx, cc):
        return (zz * 4 + xx * 2 + cc, head)

    def at_head(xx, yy):
        return (ctx, xx * 4 + yy)

    sib = at_ctx(z, xh, 1 - core)
    xhp = at_ctx(z, 1 - xh, core)
    zway = (at_ctx((z + 1) % NZ, xh, core), at_ctx((z + NZ - 1) % NZ, xh, core))
    nxt = ((ctx + 1) % 32, head)
    prv = ((ctx + 31) % 32, head)
    xp = at_head(1 - xl, y)
    yp = at_head(xl, (y + 1) % NY)
    ym = at_head(xl, (y + 3) % NY)

    bar = pltpu.get_barrier_semaphore()
    partners = [sib, xhp, zway[0], zway[1], xp, yp, ym, prv]
    for p in partners:
        pl.semaphore_signal(bar, inc=1, device_id=p, device_id_type=MESH)

    loads = []
    for i, (src, dst) in enumerate(
        ((k_ref, k), (w1_ref, w1), (w3_ref, w3), (w2_ref, w2), (rate_ref, rate), (v_ref, v),
         (q_ref, q), (gain_ref, gain), (wo_ref, wo))
    ):
        c = pltpu.make_async_copy(src, dst, load_sem.at[i])
        c.start()
        loads.append(c)

    sends = []

    def send(src, dst, ss, rs, dev):
        c = pltpu.make_async_remote_copy(
            src_ref=src, dst_ref=dst, send_sem=ss, recv_sem=rs, device_id=dev, device_id_type=MESH
        )
        c.start()
        sends.append(c)
        return c

    def arrived(dst, rs):
        pltpu.make_async_remote_copy(
            src_ref=dst, dst_ref=dst, send_sem=rs, recv_sem=rs, device_id=sib, device_id_type=MESH
        ).wait_recv()

    pieces = [
        (src, dst, blk * BL + i * HP)
        for blk in (1, 0)
        for src, dst in ((k_ref, hk), (v_ref, hv))
        for i in range(BL // HP)
    ]
    pushed = []

    def push(count):
        for _ in range(count):
            i = len(pushed)
            src, dst, lo = pieces[i]
            pushed.append(i)
            r = pl.ds(lo, HP)
            send(src.at[r], dst.at[r], halo_ss.at[i], halo_rs.at[i], nxt)

    def pulled(lo, hi):
        for i in range(lo, hi):
            src, dst, row = pieces[i]
            arrived(dst.at[pl.ds(row, HP)], halo_rs.at[i])

    for c in loads[:6]:
        c.wait()

    def grad_tile(t, carry):
        r = pl.ds(pl.multiple_of(t * TT, TT), TT)
        kt = k[r, :]
        gp = dot(kt, w1[0])
        up = dot(kt, w3[0])
        s = sigmoid(gp)
        sv = gp * s
        hid[r, :] = (sv * up).astype(BF16)
        row = rate[:, r]
        eye = lax.broadcasted_iota(jnp.int32, (TT, TT), 0) == lax.broadcasted_iota(
            jnp.int32, (TT, TT), 1
        )
        col = jnp.sum(jnp.where(eye, row, 0.0), axis=1, keepdims=True)
        tg = (-col * v[r, :].astype(F32)).astype(BF16)
        tgt[r, :] = tg
        ba = dot_nt(tg, w2[0])
        bg[r, :] = (ba * up * (s * (1.0 + gp * (1.0 - s)))).astype(BF16)
        bu[r, :] = (ba * sv).astype(BF16)
        return carry

    lax.fori_loop(0, NT, grad_tile, 0)
    pl.semaphore_wait(bar, len(partners))
    push(5)

    theirs = pl.ds(pl.multiple_of((1 - core) * HALF, HALF), HALF)
    mine = pl.ds(pl.multiple_of(core * HALF, HALF), HALF)
    pairs = ((hid, tgt), (k, bg), (k, bu))
    for m, (a, b) in enumerate(pairs):
        sib_send[m] = dot_tn(a[:, theirs], b[...]).astype(BF16)
        send(sib_send.at[m], sib_recv.at[m], sib_ss.at[m], sib_rs.at[m], sib)
    for m, (a, b) in enumerate(pairs):
        own[m] = dot_tn(a[:, mine], b[...])

    for m in range(3):
        arrived(sib_recv.at[m], sib_rs.at[m])
        own[m] = own[m] + sib_recv[m].astype(F32)

    for c in loads[6:8]:
        c.wait()
    scale = HD ** -0.5
    reach = [win_ref[0, 0], win_ref[0, 1]]

    def own_tile(t):
        r = pl.ds(t * TT, TT)
        blk = t // 2
        width = (t + 1) * TT
        s = dot_nt(q[r, :], k[pl.ds(0, width), :]) * scale
        qpos = lax.broadcasted_iota(jnp.int32, (TT, width), 0) + t * TT
        kpos = lax.broadcasted_iota(jnp.int32, (TT, width), 1)
        s = jnp.where(kpos <= qpos, s, MASKED)
        if blk == 1:
            far = jnp.where(reach[1] >= 1, 0.0, MASKED)
            s = s + jnp.where(kpos < BL, far, 0.0)
        top = jnp.max(s, axis=1, keepdims=True)
        p = jnp.exp(s - top)
        m_run[r, :] = top
        l_run[r, :] = jnp.sum(p, axis=1, keepdims=True)
        acc[r, :] = dot(p.astype(BF16), v[pl.ds(0, width), :])

    first = ctx == 0

    def halo_tile(t):
        r = pl.ds(t * TT, TT)
        blk = t // 2
        if blk == 0:
            lo, width = 0, HALO
        else:
            lo, width = BL, BL
        s = dot_nt(q[r, :], hk[pl.ds(lo, width), :]) * scale
        near = jnp.where(jnp.logical_or(reach[blk] < (1 if blk == 0 else 2), first), MASKED, 0.0)
        if blk == 0:
            far = jnp.where(jnp.logical_or(reach[blk] < 2, first), MASKED, 0.0)
            kpos = lax.broadcasted_iota(jnp.int32, (TT, width), 1)
            s = s + jnp.where(kpos < BL, far, near)
        else:
            s = s + near
        old = m_run[r, :]
        top = jnp.maximum(old, jnp.max(s, axis=1, keepdims=True))
        p = jnp.exp(s - top)
        keep = jnp.exp(old - top)
        total = l_run[r, :] * keep + jnp.sum(p, axis=1, keepdims=True)
        o = acc[r, :] * keep + dot(p.astype(BF16), hv[pl.ds(lo, width), :])
        acc[r, :] = o / total

    def shard(d):
        return pl.ds(pl.multiple_of(((z + NZ + d) % NZ) * SHARD, SHARD), SHARD)

    def goes(m, way, step):
        return step > 1 or far_way(m) == way

    for step in range(1, HOPS + 1):
        for m in range(3):
            for way in range(2):
                if not goes(m, way, step):
                    continue
                dist = HOPS + 1 - step
                part = own[m, shard(dist if way == 0 else -dist), :]
                if step > 1 and goes(m, way, step - 1):
                    arrived(rs_recv.at[m, way, step - 2], rs_rs.at[m, way, step - 2])
                    part = part + rs_recv[m, way, step - 2].astype(F32)
                rs_send[m, way, step - 1] = part.astype(BF16)
                send(
                    rs_send.at[m, way, step - 1], rs_recv.at[m, way, step - 1],
                    rs_ss.at[m, way, step - 1], rs_rs.at[m, way, step - 1], zway[way],
                )
        push(1)
        own_tile(step - 1)

    for m in range(3):
        part = own[m, shard(0), :]
        for way in range(2):
            arrived(rs_recv.at[m, way, HOPS - 1], rs_rs.at[m, way, HOPS - 1])
            part = part + rs_recv[m, way, HOPS - 1].astype(F32)
        x_send[m] = part.astype(BF16)
        send(x_send.at[m], x_recv.at[m], x_ss.at[m], x_rs.at[m], xhp)
    push(2)

    def rows_of(d, cc):
        return pl.ds(pl.multiple_of(cc * HALF + ((z + NZ + d) % NZ) * SHARD, SHARD), SHARD)

    def to_ring(m, d, way, dist):
        r = gfull.at[m, rows_of(d, core)]
        send(r, r, ag_ss.at[m, way, dist - 1], ag_rs.at[m, way, dist - 1], zway[way])

    def to_core(m, d):
        r = gfull.at[m, rows_of(d, core)]
        i = d % NZ
        send(r, r, sg_ss.at[m, i], sg_rs.at[m, i], sib)

    for m in range(3):
        arrived(x_recv.at[m], x_rs.at[m])
        both = x_send[m].astype(F32) + x_recv[m].astype(F32)
        gfull[m, rows_of(0, core), :] = both.astype(BF16)
        to_ring(m, 0, 0, 1)
        to_ring(m, 0, 1, 1)
        to_core(m, 0)

    for dist in range(1, HOPS + 1):
        for m in range(3):
            for way in range(2):
                if dist == HOPS and far_way(m) != way:
                    continue
                d = -dist if way == 0 else dist
                arrived(gfull.at[m, rows_of(d, core)], ag_rs.at[m, way, dist - 1])
                if dist + 1 < HOPS or (dist + 1 == HOPS and far_way(m) == way):
                    to_ring(m, d, way, dist + 1)
                to_core(m, d)
        if dist < HOPS:
            push((2, 2, 1)[dist - 1])

    pulled(0, len(pieces))
    for t in range(NT):
        halo_tile(t)

    squares = jnp.zeros((1, HD), F32)
    for m in range(3):
        for d in range(NZ):
            arrived(gfull.at[m, rows_of(d, 1 - core)], sg_rs.at[m, d])
        g = gfull[m].astype(F32)
        squares = squares + jnp.sum(g * g, axis=0, keepdims=True)

    gnorm = jnp.sqrt(jnp.sum(squares, axis=1, keepdims=True) + EPS)
    factor = jnp.minimum(1.0, GRAD_LIMIT / gnorm)
    for m, (old, new) in enumerate(((w2, n2), (w1, n1), (w3, n3))):
        w = old[0].astype(F32)
        u = w - factor * gfull[m].astype(F32)
        before = jnp.sqrt(jnp.sum(w * w, axis=0, keepdims=True) + EPS)
        after = jnp.sqrt(jnp.sum(u * u, axis=0, keepdims=True) + EPS)
        new[...] = (u * (before / after)).astype(BF16)

    def slot(h, t):
        return gat.at[h, pl.ds(t * GT, GT)]

    def pass_on(h, t, way):
        s = slot(h, t)
        if way == "x":
            send(s, s, gx_ss.at[t, h], g_rs.at[t, h], xp)
        elif way == "+":
            send(s, s, gy_ss.at[0, t, h], g_rs.at[t, h], yp)
        else:
            send(s, s, gy_ss.at[1, t, h], g_rs.at[t, h], ym)

    cols = [xl * 4 + (y + j) % NY for j in range(NY)]
    crss = [(1 - xl) * 4 + (y + j) % NY for j in range(NY)]

    def readout(t):
        r = pl.ds(t * TT, TT)
        qt = q[r, :]
        g = dot(qt, n1[...])
        u = dot(qt, n3[...])
        a = (g * sigmoid(g) * u).astype(BF16)
        f = dot(a, n2[...])
        ms = jnp.mean(f * f, axis=1, keepdims=True)
        nrm = f * lax.rsqrt(ms + EPS) * gain[...]
        gat[cols[0], r, :] = (nrm + acc[r, :]).astype(BF16)

    def got(h, t):
        arrived(slot(h, t), g_rs.at[t, h])

    def own_out(t):
        for way in ("x", "+", "-"):
            pass_on(cols[0], t, way)

    def one_hop(t):
        if tile_kind(t) == "A":
            got(crss[0], t)
            pass_on(crss[0], t, "+")
            pass_on(crss[0], t, "-")
            got(cols[3], t)
            pass_on(cols[3], t, "+")
            got(cols[1], t)
        else:
            plus = (t // 2) % 2 == 0
            got(cols[3], t)
            if plus:
                pass_on(cols[3], t, "+")
            pass_on(cols[3], t, "x")
            got(cols[1], t)
            if not plus:
                pass_on(cols[1], t, "-")
            pass_on(cols[1], t, "x")

    def two_hops(t):
        if tile_kind(t) == "A":
            got(crss[1], t)
            pass_on(crss[1], t, "-")
            got(crss[3], t)
            got(cols[2], t)
        else:
            got(cols[2], t)
            pass_on(cols[2], t, "x")
            got(crss[0], t)

    def rest(t):
        if tile_kind(t) == "A":
            got(crss[2], t)
        else:
            for j in (3, 1, 2):
                got(crss[j], t)

    def project(i):
        r = pl.ds(i * TT, TT)
        o = dot(gat[0, r, :], wo[pl.ds(0, HD), :])
        for h in range(1, HEADS):
            o = o + dot(gat[h, r, :], wo[pl.ds(h * HD, HD), :])
        outv[r, :] = o.astype(BF16)
        pltpu.make_async_copy(outv.at[r], out_ref.at[r], out_sem.at[i]).start()

    PER = TT // GT
    readout(0)
    own_out(0)
    readout(1)
    own_out(1)
    readout(2)
    readout(3)
    loads[8].wait()
    for step in range(1, NG + 4):
        if step - 1 < NG:
            one_hop(step - 1)
        if 0 <= step - 2 < NG:
            two_hops(step - 2)
        if step + 1 < NG:
            own_out(step + 1)
        if 0 <= step - 4 < NG:
            t = step - 4
            rest(t)
            if (t + 1) % PER == 0:
                project(t // PER)

    for i in range(NT):
        r = pl.ds(i * TT, TT)
        pltpu.make_async_copy(outv.at[r], out_ref.at[r], out_sem.at[i]).wait()
    for c in sends:
        c.wait_send()


def per_device(*args):
    any_spec = pl.BlockSpec(memory_space=pl.ANY)
    in_specs = [any_spec] * 10
    in_specs[4] = pl.BlockSpec(memory_space=pltpu.SMEM)
    V = pltpu.VMEM
    D = pltpu.SemaphoreType.DMA
    scratch = [
        V((TOK, HD), BF16), V((TOK, HD), BF16), V((TOK, HD), BF16),
        V((HALO, HD), BF16), V((HALO, HD), BF16),
        V((1, HD, HD), BF16), V((1, HD, HD), BF16), V((1, HD, HD), BF16),
        V((HEADS * HD, COLS), BF16), V((1, TOK), F32), V((1, HD), F32),
        V((TOK, HD), BF16), V((TOK, HD), BF16), V((TOK, HD), BF16), V((TOK, HD), BF16),
        V((3, HALF, HD), BF16), V((3, HALF, HD), BF16), V((3, HALF, HD), F32),
        V((3, 2, HOPS, SHARD, HD), BF16), V((3, 2, HOPS, SHARD, HD), BF16),
        V((3, SHARD, HD), BF16), V((3, SHARD, HD), BF16), V((3, HD, HD), BF16),
        V((HD, HD), BF16), V((HD, HD), BF16), V((HD, HD), BF16),
        V((TOK, 1), F32), V((TOK, 1), F32), V((TOK, HD), F32),
        V((HEADS, TOK, HD), BF16), V((TOK, COLS), BF16),
        D((9,)), D((NT,)), D((16,)), D((16,)), D((3,)), D((3,)),
        D((3, 2, HOPS)), D((3, 2, HOPS)), D((3,)), D((3,)),
        D((3, 2, HOPS)), D((3, 2, HOPS)), D((3, NZ)), D((3, NZ)),
        D((2, NG, HEADS)), D((NG, HEADS)), D((NG, HEADS)),
    ]
    return pl.pallas_call(
        body,
        out_shape=jax.ShapeDtypeStruct((TOK, COLS), BF16),
        in_specs=in_specs,
        out_specs=any_spec,
        scratch_shapes=scratch,
        compiler_params=pltpu.CompilerParams(
            collective_id=0, has_side_effects=True, vmem_limit_bytes=60 << 20
        ),
        cost_estimate=pl.CostEstimate(flops=13_400_000_000, bytes_accessed=15_000_000, transcendentals=3_000_000),
        name="ttt_layer",
    )(*args)


def solution(mesh):
    placed = (
        P("ctx", "head"),
        P("ctx", "head"),
        P("ctx", "head"),
        P("head", "ctx"),
        P("head", "ctx"),
        P("head", None, None),
        P("head", None, None),
        P("head", None, None),
        P("head", None),
        P(None, "head"),
    )
    return jax.shard_map(
        per_device, mesh=mesh, in_specs=placed, out_specs=P("ctx", "head"), check_vma=False
    )
```

```python
import jax
import jax.numpy as jnp
from jax import lax
from jax.sharding import PartitionSpec as P
from jax.experimental import pallas as pl
from jax.experimental.pallas import tpu as pltpu

MESH = pl.DeviceIdType.MESH
F32 = jnp.float32
BF16 = jnp.bfloat16

TOK = 1024
HD = 512
BL = 512
HALO = 1024
NZ = 8
NY = 4
HEADS = 8
COLS = 640
HALF = 256
SHARD = 32
HOPS = NZ // 2
TT = 256
NT = TOK // TT
MY = TOK // 2
GT = 64
NG = MY // GT
PT = 128
NP = MY // PT
WP = HEADS // 2
HP = 128
GRAD_LIMIT = 24.0
EPS = 1e-6
MASKED = -1e30


def sigmoid(x):
    return 0.5 * jnp.tanh(0.5 * x) + 0.5


def dot(a, b):
    return jnp.dot(a, b, preferred_element_type=F32)


def dot_nt(a, b):
    return lax.dot_general(a, b, (((1,), (1,)), ((), ())), preferred_element_type=F32)


def dot_tn(a, b):
    return lax.dot_general(a, b, (((0,), (0,)), ((), ())), preferred_element_type=F32)


def far_way(m):
    return m % 2


def body(
    q_ref, k_ref, v_ref, rate_ref, win_ref, w1_ref, w3_ref, w2_ref, gain_ref, wo_ref,
    out_ref,
    q, k, v, hk, hv, stage, w1, w3, w2, wo, rate, gain,
    hid, tgt, bg, bu,
    sib_send, sib_recv, own, rs_send, rs_recv, x_send, x_recv, gfull,
    n1, n3, n2, m_run, l_run, acc, gat, oth, wo2, sum_here, sum_pair, opair, outv,
    load_sem, out_sem, halo_ss, halo_rs, stage_ss, stage_rs, sib_ss, sib_rs, rs_ss, rs_rs, x_ss, x_rs,
    ag_ss, ag_rs, sg_ss, sg_rs, g_ss, g_rs, w_ss, w_rs, ws_ss, ws_rs, o_ss, o_rs,
):
    ctx = lax.axis_index("ctx")
    head = lax.axis_index("head")
    z = ctx // 4
    xh = (ctx // 2) % 2
    core = ctx % 2
    xl = head // 4
    y = head % 4

    def at_ctx(zz, xx, cc):
        return (zz * 4 + xx * 2 + cc, head)

    def at_head(xx, yy):
        return (ctx, xx * 4 + yy)

    sib = at_ctx(z, xh, 1 - core)
    xhp = at_ctx(z, 1 - xh, core)
    zway = (at_ctx((z + 1) % NZ, xh, core), at_ctx((z + NZ - 1) % NZ, xh, core))
    nxt = ((ctx + 1) % 32, head)
    prv = ((ctx + 31) % 32, head)
    over = at_ctx((z + 1) % NZ, xh, 1 - core)
    under = at_ctx((z + NZ - 1) % NZ, xh, 1 - core)
    crosses = jnp.logical_and(core == 1, xh == 1)
    relays = jnp.logical_and(core == 1, xh == 0)
    xp = at_head(1 - xl, y)
    group = y // 2
    y_pair = 3 - y
    y_mate = 1 - y + 4 * group
    y_far = 3 - y_mate
    pair = at_head(xl, y_pair)
    mate = at_head(xl, y_mate)

    bar = pltpu.get_barrier_semaphore()
    partners = [sib, xhp, zway[0], zway[1], xp, pair, mate, prv, under]
    for p in partners:
        pl.semaphore_signal(bar, inc=1, device_id=p, device_id_type=MESH)

    loads = []
    for i, (src, dst) in enumerate(
        ((k_ref, k), (w1_ref, w1), (w3_ref, w3), (w2_ref, w2), (rate_ref, rate), (v_ref, v),
         (q_ref, q), (gain_ref, gain), (wo_ref, wo))
    ):
        c = pltpu.make_async_copy(src, dst, load_sem.at[i])
        if i < 6:
            c.start()
        loads.append(c)

    sends = []

    def copy(src, dst, ss, rs, dev):
        return pltpu.make_async_remote_copy(
            src_ref=src, dst_ref=dst, send_sem=ss, recv_sem=rs, device_id=dev, device_id_type=MESH
        )

    def send(src, dst, ss, rs, dev):
        c = copy(src, dst, ss, rs, dev)
        c.start()
        sends.append(c)
        return c

    def arrived(dst, rs):
        pltpu.make_async_remote_copy(
            src_ref=dst, dst_ref=dst, send_sem=rs, recv_sem=rs, device_id=sib, device_id_type=MESH
        ).wait_recv()

    pieces = [
        (src, dst, blk * BL + i * HP)
        for blk in (1, 0)
        for i in range(BL // HP)
        for src, dst in ((v_ref, hv), (k_ref, hk))
    ]
    pushed = []
    passed = []

    def push(count):
        for _ in range(count):
            i = len(pushed)
            src, dst, lo = pieces[i]
            pushed.append(i)
            r = pl.ds(lo, HP)
            if dst is hk:
                send(src.at[r], dst.at[r], halo_ss.at[i], halo_rs.at[i], nxt)
                continue

            c = copy(src.at[r], dst.at[r], halo_ss.at[i], halo_rs.at[i], nxt)
            first_leg = copy(src.at[r], stage.at[r], halo_ss.at[i], stage_rs.at[i], xhp)
            sends.append(c)

            @pl.when(jnp.logical_not(crosses))
            def _():
                c.start()

            @pl.when(crosses)
            def _():
                first_leg.start()

    def pass_values(count):
        for _ in range(count):
            i = 2 * len(passed)
            src, dst, lo = pieces[i]
            r = pl.ds(lo, HP)
            c = copy(stage.at[r], dst.at[r], stage_ss.at[i], halo_rs.at[i], over)
            passed.append(c)

            @pl.when(relays)
            def _():
                arrived(stage.at[r], stage_rs.at[i])
                c.start()

    def pulled(lo, hi):
        for i in range(lo, hi):
            src, dst, row = pieces[i]
            arrived(dst.at[pl.ds(row, HP)], halo_rs.at[i])

    for c in loads[:6]:
        c.wait()
    for c in loads[6:]:
        c.start()

    def grad_tile(t, carry):
        r = pl.ds(pl.multiple_of(t * TT, TT), TT)
        kt = k[r, :]
        gp = dot(kt, w1[0])
        up = dot(kt, w3[0])
        s = sigmoid(gp)
        sv = gp * s
        hid[r, :] = (sv * up).astype(BF16)
        row = rate[:, r]
        eye = lax.broadcasted_iota(jnp.int32, (TT, TT), 0) == lax.broadcasted_iota(
            jnp.int32, (TT, TT), 1
        )
        col = jnp.sum(jnp.where(eye, row, 0.0), axis=1, keepdims=True)
        tg = (-col * v[r, :].astype(F32)).astype(BF16)
        tgt[r, :] = tg
        ba = dot_nt(tg, w2[0])
        bg[r, :] = (ba * up * (s * (1.0 + gp * (1.0 - s)))).astype(BF16)
        bu[r, :] = (ba * sv).astype(BF16)
        return carry

    lax.fori_loop(0, 2, grad_tile, 0)
    pl.semaphore_wait(bar, len(partners))
    push(6)

    def w_rows(cc, i):
        return pl.ds(pl.multiple_of((cc * WP + i) * HD, HD), HD)

    for i in range(WP):
        r = w_rows(core, i)
        send(wo_ref.at[r], wo2.at[r], w_ss.at[i], w_rs.at[i], pair)

    lax.fori_loop(2, NT, grad_tile, 0)
    push(3)

    def w_on(i):
        r = wo2.at[w_rows(core, i)]
        arrived(r, w_rs.at[i])
        send(r, r, ws_ss.at[i], ws_rs.at[i], sib)


    theirs = pl.ds(pl.multiple_of((1 - core) * HALF, HALF), HALF)
    mine = pl.ds(pl.multiple_of(core * HALF, HALF), HALF)
    pairs = ((hid, tgt), (k, bg), (k, bu))
    for m, (a, b) in enumerate(pairs):
        sib_send[m] = dot_tn(a[:, theirs], b[...]).astype(BF16)
        send(sib_send.at[m], sib_recv.at[m], sib_ss.at[m], sib_rs.at[m], sib)
    for m, (a, b) in enumerate(pairs):
        own[m] = dot_tn(a[:, mine], b[...])

    for m in range(3):
        arrived(sib_recv.at[m], sib_rs.at[m])
        own[m] = own[m] + sib_recv[m].astype(F32)

    for c in loads[6:8]:
        c.wait()
    scale = HD ** -0.5
    reach = [win_ref[0, 0], win_ref[0, 1]]

    def own_tile(t):
        r = pl.ds(t * TT, TT)
        blk = t // 2
        width = (t + 1) * TT
        s = dot_nt(q[r, :], k[pl.ds(0, width), :]) * scale
        qpos = lax.broadcasted_iota(jnp.int32, (TT, width), 0) + t * TT
        kpos = lax.broadcasted_iota(jnp.int32, (TT, width), 1)
        s = jnp.where(kpos <= qpos, s, MASKED)
        if blk == 1:
            far = jnp.where(reach[1] >= 1, 0.0, MASKED)
            s = s + jnp.where(kpos < BL, far, 0.0)
        top = jnp.max(s, axis=1, keepdims=True)
        p = jnp.exp(s - top)
        m_run[r, :] = top
        l_run[r, :] = jnp.sum(p, axis=1, keepdims=True)
        acc[r, :] = dot(p.astype(BF16), v[pl.ds(0, width), :])

    first = ctx == 0

    def halo_tile(t):
        r = pl.ds(t * TT, TT)
        blk = t // 2
        if blk == 0:
            lo, width = 0, HALO
        else:
            lo, width = BL, BL
        s = dot_nt(q[r, :], hk[pl.ds(lo, width), :]) * scale
        near = jnp.where(jnp.logical_or(reach[blk] < (1 if blk == 0 else 2), first), MASKED, 0.0)
        if blk == 0:
            far = jnp.where(jnp.logical_or(reach[blk] < 2, first), MASKED, 0.0)
            kpos = lax.broadcasted_iota(jnp.int32, (TT, width), 1)
            s = s + jnp.where(kpos < BL, far, near)
        else:
            s = s + near
        old = m_run[r, :]
        top = jnp.maximum(old, jnp.max(s, axis=1, keepdims=True))
        p = jnp.exp(s - top)
        keep = jnp.exp(old - top)
        total = l_run[r, :] * keep + jnp.sum(p, axis=1, keepdims=True)
        o = acc[r, :] * keep + dot(p.astype(BF16), hv[pl.ds(lo, width), :])
        acc[r, :] = o / total

    def shard(d):
        return pl.ds(pl.multiple_of(((z + NZ + d) % NZ) * SHARD, SHARD), SHARD)

    def goes(m, way, step):
        return step > 1 or far_way(m) == way

    for step in range(1, HOPS + 1):
        for m in range(3):
            for way in range(2):
                if not goes(m, way, step):
                    continue
                dist = HOPS + 1 - step
                part = own[m, shard(dist if way == 0 else -dist), :]
                if step > 1 and goes(m, way, step - 1):
                    arrived(rs_recv.at[m, way, step - 2], rs_rs.at[m, way, step - 2])
                    part = part + rs_recv[m, way, step - 2].astype(F32)
                rs_send[m, way, step - 1] = part.astype(BF16)
                send(
                    rs_send.at[m, way, step - 1], rs_recv.at[m, way, step - 1],
                    rs_ss.at[m, way, step - 1], rs_rs.at[m, way, step - 1], zway[way],
                )
        push(1)
        pass_values(2 if step == 1 else 1)
        own_tile(step - 1)

    for m in range(3):
        part = own[m, shard(0), :]
        for way in range(2):
            arrived(rs_recv.at[m, way, HOPS - 1], rs_rs.at[m, way, HOPS - 1])
            part = part + rs_recv[m, way, HOPS - 1].astype(F32)
        x_send[m] = part.astype(BF16)
        send(x_send.at[m], x_recv.at[m], x_ss.at[m], x_rs.at[m], xhp)
    push(2)
    pass_values(1)

    def rows_of(d, cc):
        return pl.ds(pl.multiple_of(cc * HALF + ((z + NZ + d) % NZ) * SHARD, SHARD), SHARD)

    def to_ring(m, d, way, dist):
        r = gfull.at[m, rows_of(d, core)]
        send(r, r, ag_ss.at[m, way, dist - 1], ag_rs.at[m, way, dist - 1], zway[way])

    def to_core(m, d):
        r = gfull.at[m, rows_of(d, core)]
        i = d % NZ
        send(r, r, sg_ss.at[m, i], sg_rs.at[m, i], sib)

    for m in range(3):
        arrived(x_recv.at[m], x_rs.at[m])
        both = x_send[m].astype(F32) + x_recv[m].astype(F32)
        gfull[m, rows_of(0, core), :] = both.astype(BF16)
        to_ring(m, 0, 0, 1)
        to_ring(m, 0, 1, 1)
        to_core(m, 0)

    for dist in range(1, HOPS + 1):
        for m in range(3):
            for way in range(2):
                if dist == HOPS and far_way(m) != way:
                    continue
                d = -dist if way == 0 else dist
                arrived(gfull.at[m, rows_of(d, core)], ag_rs.at[m, way, dist - 1])
                if dist + 1 < HOPS or (dist + 1 == HOPS and far_way(m) == way):
                    to_ring(m, d, way, dist + 1)
                to_core(m, d)
        if dist < 3:
            push(2 - dist)
            pass_values(1)

    w_on(0)
    w_on(1)
    pulled(0, len(pieces))
    for t in range(NT):
        halo_tile(t)

    squares = jnp.zeros((1, HD), F32)
    for m in range(3):
        for d in range(NZ):
            arrived(gfull.at[m, rows_of(d, 1 - core)], sg_rs.at[m, d])
        g = gfull[m].astype(F32)
        squares = squares + jnp.sum(g * g, axis=0, keepdims=True)

    gnorm = jnp.sqrt(jnp.sum(squares, axis=1, keepdims=True) + EPS)
    factor = jnp.minimum(1.0, GRAD_LIMIT / gnorm)
    for m, (old, new) in enumerate(((w2, n2), (w1, n1), (w3, n3))):
        w = old[0].astype(F32)
        u = w - factor * gfull[m].astype(F32)
        before = jnp.sqrt(jnp.sum(w * w, axis=0, keepdims=True) + EPS)
        after = jnp.sqrt(jnp.sum(u * u, axis=0, keepdims=True) + EPS)
        new[...] = (u * (before / after)).astype(BF16)

    h_own = head
    h_mate = xl * 4 + y_mate
    h_pair = xl * 4 + y_pair
    h_far = xl * 4 + y_far
    x_own = (1 - xl) * 4 + y
    x_mate = (1 - xl) * 4 + y_mate
    x_pair = (1 - xl) * 4 + y_pair
    x_far = (1 - xl) * 4 + y_far

    def readout(half, i):
        r = pl.ds(pl.multiple_of(half * MY + i * TT, TT), TT)
        qt = q[r, :]
        g = dot(qt, n1[...])
        u = dot(qt, n3[...])
        a = (g * sigmoid(g) * u).astype(BF16)
        f = dot(a, n2[...])
        ms = jnp.mean(f * f, axis=1, keepdims=True)
        nrm = f * lax.rsqrt(ms + EPS) * gain[...]
        return (nrm + acc[r, :]).astype(BF16)

    def slot(h, t):
        return gat.at[h, pl.ds(t * GT, GT)]

    def got(h, t):
        arrived(slot(h, t), g_rs.at[t, h])

    def pass_on(h, t, kind, dev):
        send(slot(h, t), slot(h, t), g_ss.at[t, kind], g_rs.at[t, h], dev)

    def own_out(t):
        pass_on(h_own, t, 0, xp)
        pass_on(h_own, t, 1, mate)

    def other_out(t):
        send(oth.at[pl.ds(t * GT, GT)], slot(h_own, t), g_ss.at[t, 2], g_rs.at[t, h_own], pair)

    def near_one(t):
        if t % 2 == 0:
            got(x_own, t)
            pass_on(x_own, t, 3, mate)
        else:
            got(h_mate, t)
            pass_on(h_mate, t, 3, xp)

    def near_rest(t):
        got(h_mate if t % 2 == 0 else x_own, t)
        got(x_mate, t)

    def pair_one(t):
        got(h_pair, t)
        pass_on(h_pair, t, 4, mate)
        pass_on(h_pair, t, 5, xp)

    def pair_two(t):
        if t % 2 == 0:
            got(h_far, t)
            pass_on(h_far, t, 6, xp)
        else:
            got(x_pair, t)
            pass_on(x_pair, t, 6, mate)

    def pair_rest(t):
        got(x_pair if t % 2 == 0 else h_far, t)
        got(x_far, t)

    def heads_dot(heads, r, w):
        o = None
        for h in heads:
            p = dot(gat[h, r, :], w[pl.ds(pl.multiple_of(h * HD, HD), HD), :])
            o = p if o is None else o + p
        return o

    near = (h_own, h_mate, x_own, x_mate)
    distant = (h_pair, h_far, x_pair, x_far)

    def project(i):
        r = pl.ds(i * PT, PT)
        here = pl.ds(pl.multiple_of(group * MY + i * PT, PT), PT)
        opair[r, :] = (sum_pair[r, :] + heads_dot(distant, r, wo2)).astype(BF16)
        send(opair.at[r], outv.at[here], o_ss.at[i], o_rs.at[i], pair)
        outv[here, :] = (sum_here[r, :] + heads_dot(distant, r, wo)).astype(BF16)
        pltpu.make_async_copy(outv.at[here], out_ref.at[here], out_sem.at[0, i]).start()

    for i in range(MY // TT):
        r = pl.ds(i * TT, TT)
        gat[h_own, r, :] = readout(group, i)
        for t in range(i * TT // GT, (i + 1) * TT // GT):
            own_out(t)
        oth[r, :] = readout(1 - group, i)
        for t in range(i * TT // GT, (i + 1) * TT // GT):
            other_out(t)
    w_on(2)
    loads[8].wait()

    def sum_up(i):
        r = pl.ds(i * TT, TT)
        sum_here[r, :] = heads_dot(near, r, wo)

    def sum_up_pair(i):
        r = pl.ds(i * TT, TT)
        sum_pair[r, :] = heads_dot(near, r, wo2)

    for t in range(NG):
        near_one(t)
    w_on(3)
    for t in (0, 1):
        pair_one(t)
    for t in range(4):
        near_rest(t)
    sum_up(0)
    for t in (2, 3):
        pair_one(t)
    for t in (0, 1):
        pair_two(t)
    for t in range(4, 8):
        near_rest(t)
    sum_up(1)
    for t in (4, 5):
        pair_one(t)
    for t in (2, 3):
        pair_two(t)
    for i in range(WP):
        arrived(wo2.at[w_rows(1 - core, i)], ws_rs.at[i])
    sum_up_pair(0)
    for t in (6, 7):
        pair_one(t)
    for t in (4, 5):
        pair_two(t)
    sum_up_pair(1)
    for t in (0, 1):
        pair_rest(t)
    project(0)
    for t in (6, 7):
        pair_two(t)
    for i in range(1, NP):
        for t in (2 * i, 2 * i + 1):
            pair_rest(t)
        project(i)

    for i in range(NP):
        there = pl.ds(pl.multiple_of((1 - group) * MY + i * PT, PT), PT)
        arrived(outv.at[there], o_rs.at[i])
        pltpu.make_async_copy(outv.at[there], out_ref.at[there], out_sem.at[1, i]).start()
    for i in range(NP):
        for j in range(2):
            half = group if j == 0 else 1 - group
            r = pl.ds(pl.multiple_of(half * MY + i * PT, PT), PT)
            pltpu.make_async_copy(outv.at[r], out_ref.at[r], out_sem.at[j, i]).wait()
    for c in sends:
        c.wait_send()

    @pl.when(relays)
    def _():
        for c in passed:
            c.wait_send()


def per_device(*args):
    any_spec = pl.BlockSpec(memory_space=pl.ANY)
    in_specs = [any_spec] * 10
    in_specs[4] = pl.BlockSpec(memory_space=pltpu.SMEM)
    V = pltpu.VMEM
    D = pltpu.SemaphoreType.DMA
    scratch = [
        V((TOK, HD), BF16), V((TOK, HD), BF16), V((TOK, HD), BF16),
        V((HALO, HD), BF16), V((HALO, HD), BF16), V((HALO, HD), BF16),
        V((1, HD, HD), BF16), V((1, HD, HD), BF16), V((1, HD, HD), BF16),
        V((HEADS * HD, COLS), BF16), V((1, TOK), F32), V((1, HD), F32),
        V((TOK, HD), BF16), V((TOK, HD), BF16), V((TOK, HD), BF16), V((TOK, HD), BF16),
        V((3, HALF, HD), BF16), V((3, HALF, HD), BF16), V((3, HALF, HD), F32),
        V((3, 2, HOPS, SHARD, HD), BF16), V((3, 2, HOPS, SHARD, HD), BF16),
        V((3, SHARD, HD), BF16), V((3, SHARD, HD), BF16), V((3, HD, HD), BF16),
        V((HD, HD), BF16), V((HD, HD), BF16), V((HD, HD), BF16),
        V((TOK, 1), F32), V((TOK, 1), F32), V((TOK, HD), F32),
        V((HEADS, MY, HD), BF16), V((MY, HD), BF16),
        V((HEADS * HD, COLS), BF16), V((MY, COLS), F32), V((MY, COLS), F32),
        V((MY, COLS), BF16), V((TOK, COLS), BF16),
        D((9,)), D((2, NP)), D((16,)), D((16,)), D((16,)), D((16,)), D((3,)), D((3,)),
        D((3, 2, HOPS)), D((3, 2, HOPS)), D((3,)), D((3,)),
        D((3, 2, HOPS)), D((3, 2, HOPS)), D((3, NZ)), D((3, NZ)),
        D((NG, 7)), D((NG, HEADS)), D((WP,)), D((WP,)), D((WP,)), D((WP,)), D((NP,)), D((NP,)),
    ]
    return pl.pallas_call(
        body,
        out_shape=jax.ShapeDtypeStruct((TOK, COLS), BF16),
        in_specs=in_specs,
        out_specs=any_spec,
        scratch_shapes=scratch,
        compiler_params=pltpu.CompilerParams(
            collective_id=0, has_side_effects=True, vmem_limit_bytes=60 << 20
        ),
        cost_estimate=pl.CostEstimate(flops=13_400_000_000, bytes_accessed=15_000_000, transcendentals=3_000_000),
        name="ttt_layer",
    )(*args)


def solution(mesh):
    placed = (
        P("ctx", "head"),
        P("ctx", "head"),
        P("ctx", "head"),
        P("head", "ctx"),
        P("head", "ctx"),
        P("head", None, None),
        P("head", None, None),
        P("head", None, None),
        P("head", None),
        P(None, "head"),
    )
    return jax.shard_map(
        per_device, mesh=mesh, in_specs=placed, out_specs=P("ctx", "head"), check_vma=False
    )
```

```python
import jax
import jax.numpy as jnp
from jax import lax
from jax.sharding import PartitionSpec as P
from jax.experimental import pallas as pl
from jax.experimental.pallas import tpu as pltpu

MESH = pl.DeviceIdType.MESH
F32 = jnp.float32
BF16 = jnp.bfloat16

TOK = 1024
HD = 512
BL = 512
HALO = 1024
NZ = 8
NY = 4
HEADS = 8
COLS = 640
HALF = 256
SHARD = 32
HOPS = NZ // 2
TT = 256
NT = TOK // TT
MY = TOK // 2
GT = 64
NG = MY // GT
PT = 128
NP = MY // PT
OUT_PARTS = ((0, 128), (128, 128), (256, 128), (384, 64), (448, 64))
WP = HEADS // 2
ONE_LAG = 0
TWO_LAG = 2
HP = 128
GRAD_LIMIT = 24.0
EPS = 1e-6
MASKED = -1e30


def sigmoid(x):
    return 0.5 * jnp.tanh(0.5 * x) + 0.5


def dot(a, b):
    return jnp.dot(a, b, preferred_element_type=F32)


def dot_nt(a, b):
    return lax.dot_general(a, b, (((1,), (1,)), ((), ())), preferred_element_type=F32)


def dot_tn(a, b):
    return lax.dot_general(a, b, (((0,), (0,)), ((), ())), preferred_element_type=F32)


def far_way(m):
    return m % 2


def body(
    q_ref, k_ref, v_ref, rate_ref, win_ref, w1_ref, w3_ref, w2_ref, gain_ref, wo_ref,
    out_ref,
    q, k, v, hk, hv, stage, w1, w3, w2, wo, rate, gain,
    hid, tgt, bg, bu,
    sib_send, sib_recv, own, rs_send, rs_recv, x_send, x_recv, gfull,
    n1, n3, n2, m_run, l_run, acc, gat, oth, wo2, opair, outv,
    load_sem, out_sem, halo_ss, halo_rs, stage_ss, stage_rs, sib_ss, sib_rs, rs_ss, rs_rs, x_ss, x_rs,
    ag_ss, ag_rs, sg_ss, sg_rs, g_ss, g_rs, w_ss, w_rs, ws_ss, ws_rs, o_ss, o_rs,
):
    ctx = lax.axis_index("ctx")
    head = lax.axis_index("head")
    z = ctx // 4
    xh = (ctx // 2) % 2
    core = ctx % 2
    xl = head // 4
    y = head % 4

    def at_ctx(zz, xx, cc):
        return (zz * 4 + xx * 2 + cc, head)

    def at_head(xx, yy):
        return (ctx, xx * 4 + yy)

    sib = at_ctx(z, xh, 1 - core)
    xhp = at_ctx(z, 1 - xh, core)
    zway = (at_ctx((z + 1) % NZ, xh, core), at_ctx((z + NZ - 1) % NZ, xh, core))
    nxt = ((ctx + 1) % 32, head)
    prv = ((ctx + 31) % 32, head)
    over = at_ctx((z + 1) % NZ, xh, 1 - core)
    under = at_ctx((z + NZ - 1) % NZ, xh, 1 - core)
    crosses = jnp.logical_and(core == 1, xh == 1)
    relays = jnp.logical_and(core == 1, xh == 0)
    xp = at_head(1 - xl, y)
    group = y // 2
    y_pair = 3 - y
    y_mate = 1 - y + 4 * group
    y_far = 3 - y_mate
    pair = at_head(xl, y_pair)
    mate = at_head(xl, y_mate)

    bar = pltpu.get_barrier_semaphore()
    partners = [sib, xhp, zway[0], zway[1], xp, pair, mate, prv, under]
    for p in partners:
        pl.semaphore_signal(bar, inc=1, device_id=p, device_id_type=MESH)

    loads = []
    lo, hi = pl.ds(0, TOK // 2), pl.ds(TOK // 2, TOK // 2)
    for i, (src, dst) in enumerate(
        ((k_ref.at[lo], k.at[lo]), (w1_ref, w1), (w3_ref, w3), (rate_ref, rate),
         (v_ref.at[lo], v.at[lo]), (w2_ref, w2), (k_ref.at[hi], k.at[hi]), (v_ref.at[hi], v.at[hi]),
         (q_ref, q), (gain_ref, gain), (wo_ref, wo))
    ):
        c = pltpu.make_async_copy(src, dst, load_sem.at[i])
        if i < 8:
            c.start()
        loads.append(c)

    sends = []

    def copy(src, dst, ss, rs, dev):
        return pltpu.make_async_remote_copy(
            src_ref=src, dst_ref=dst, send_sem=ss, recv_sem=rs, device_id=dev, device_id_type=MESH
        )

    def send(src, dst, ss, rs, dev):
        c = copy(src, dst, ss, rs, dev)
        c.start()
        sends.append(c)
        return c

    def arrived(dst, rs):
        pltpu.make_async_remote_copy(
            src_ref=dst, dst_ref=dst, send_sem=rs, recv_sem=rs, device_id=sib, device_id_type=MESH
        ).wait_recv()

    pieces = [
        (src, dst, blk * BL + i * HP)
        for blk in (1, 0)
        for i in range(BL // HP)
        for src, dst in ((v_ref, hv), (k_ref, hk))
    ]
    pushed = []
    passed = []

    def push(count):
        for _ in range(count):
            i = len(pushed)
            src, dst, lo = pieces[i]
            pushed.append(i)
            r = pl.ds(lo, HP)
            if dst is hk:
                send(src.at[r], dst.at[r], halo_ss.at[i], halo_rs.at[i], nxt)
                continue

            c = copy(src.at[r], dst.at[r], halo_ss.at[i], halo_rs.at[i], nxt)
            first_leg = copy(src.at[r], stage.at[r], halo_ss.at[i], stage_rs.at[i], xhp)
            sends.append(c)

            @pl.when(jnp.logical_not(crosses))
            def _():
                c.start()

            @pl.when(crosses)
            def _():
                first_leg.start()

    def pass_values(count):
        for _ in range(count):
            i = 2 * len(passed)
            src, dst, lo = pieces[i]
            r = pl.ds(lo, HP)
            c = copy(stage.at[r], dst.at[r], stage_ss.at[i], halo_rs.at[i], over)
            passed.append(c)

            @pl.when(relays)
            def _():
                arrived(stage.at[r], stage_rs.at[i])
                c.start()

    def pulled(lo, hi):
        for i in range(lo, hi):
            src, dst, row = pieces[i]
            arrived(dst.at[pl.ds(row, HP)], halo_rs.at[i])

    for c in loads[:6]:
        c.wait()

    def grad_tile(t, carry):
        r = pl.ds(pl.multiple_of(t * TT, TT), TT)
        kt = k[r, :]
        gp = dot(kt, w1[0])
        up = dot(kt, w3[0])
        s = sigmoid(gp)
        sv = gp * s
        hid[r, :] = (sv * up).astype(BF16)
        row = rate[:, r]
        eye = lax.broadcasted_iota(jnp.int32, (TT, TT), 0) == lax.broadcasted_iota(
            jnp.int32, (TT, TT), 1
        )
        col = jnp.sum(jnp.where(eye, row, 0.0), axis=1, keepdims=True)
        tg = (-col * v[r, :].astype(F32)).astype(BF16)
        tgt[r, :] = tg
        ba = dot_nt(tg, w2[0])
        bg[r, :] = (ba * up * (s * (1.0 + gp * (1.0 - s)))).astype(BF16)
        bu[r, :] = (ba * sv).astype(BF16)
        return carry

    lax.fori_loop(0, 2, grad_tile, 0)
    pl.semaphore_wait(bar, len(partners))
    push(6)

    keep = 2 + z % 2
    lack = 3 - z % 2
    half_rows = HD // 2

    def w_at(cc, i, lo=0, n=HD):
        return wo2.at[pl.ds(pl.multiple_of((cc * WP + i) * HD + lo, half_rows), n)]

    def w_part(cc, j):
        return (
            w_at(cc, keep), w_at(cc, 0), w_at(cc, 1),
            w_at(cc, lack, 0, half_rows), w_at(cc, lack, half_rows, half_rows),
        )[j]

    for j, i in enumerate((keep, 0, 1)):
        r = pl.ds(pl.multiple_of((core * WP + i) * HD, HD), HD)
        send(wo_ref.at[r], wo2.at[r], w_ss.at[j], w_rs.at[j], pair)

    def w_swap():
        for way in range(2):
            r = w_at(core, keep, way * half_rows, half_rows)
            send(r, r, w_ss.at[3 + way], w_rs.at[3 + way], zway[way])

    for c in loads[6:8]:
        c.wait()
    for c in loads[8:]:
        c.start()
    lax.fori_loop(2, NT, grad_tile, 0)
    push(3)

    def w_on(j):
        r = w_part(core, j)
        arrived(r, w_rs.at[j])
        send(r, r, ws_ss.at[j], ws_rs.at[j], sib)

    theirs = pl.ds(pl.multiple_of((1 - core) * HALF, HALF), HALF)
    mine = pl.ds(pl.multiple_of(core * HALF, HALF), HALF)
    pairs = ((hid, tgt), (k, bg), (k, bu))
    for m, (a, b) in enumerate(pairs):
        sib_send[m] = dot_tn(a[:, theirs], b[...]).astype(BF16)
        send(sib_send.at[m], sib_recv.at[m], sib_ss.at[m], sib_rs.at[m], sib)

    for c in loads[8:10]:
        c.wait()
    scale = HD ** -0.5
    reach = [win_ref[0, 0], win_ref[0, 1]]

    def own_tile(t):
        r = pl.ds(t * TT, TT)
        blk = t // 2
        width = (t + 1) * TT
        s = dot_nt(q[r, :], k[pl.ds(0, width), :]) * scale
        qpos = lax.broadcasted_iota(jnp.int32, (TT, width), 0) + t * TT
        kpos = lax.broadcasted_iota(jnp.int32, (TT, width), 1)
        s = jnp.where(kpos <= qpos, s, MASKED)
        if blk == 1:
            far = jnp.where(reach[1] >= 1, 0.0, MASKED)
            s = s + jnp.where(kpos < BL, far, 0.0)
        top = jnp.max(s, axis=1, keepdims=True)
        p = jnp.exp(s - top)
        m_run[r, :] = top
        l_run[r, :] = jnp.sum(p, axis=1, keepdims=True)
        acc[r, :] = dot(p.astype(BF16), v[pl.ds(0, width), :])

    first = ctx == 0

    def halo_tile(t):
        r = pl.ds(t * TT, TT)
        blk = t // 2
        if blk == 0:
            lo, width = 0, HALO
        else:
            lo, width = BL, BL
        s = dot_nt(q[r, :], hk[pl.ds(lo, width), :]) * scale
        near = jnp.where(jnp.logical_or(reach[blk] < (1 if blk == 0 else 2), first), MASKED, 0.0)
        if blk == 0:
            far = jnp.where(jnp.logical_or(reach[blk] < 2, first), MASKED, 0.0)
            kpos = lax.broadcasted_iota(jnp.int32, (TT, width), 1)
            s = s + jnp.where(kpos < BL, far, near)
        else:
            s = s + near
        old = m_run[r, :]
        top = jnp.maximum(old, jnp.max(s, axis=1, keepdims=True))
        p = jnp.exp(s - top)
        keep = jnp.exp(old - top)
        total = l_run[r, :] * keep + jnp.sum(p, axis=1, keepdims=True)
        o = acc[r, :] * keep + dot(p.astype(BF16), hv[pl.ds(lo, width), :])
        acc[r, :] = o / total

    def shard(d):
        return pl.ds(pl.multiple_of(((z + NZ + d) % NZ) * SHARD, SHARD), SHARD)

    def goes(m, way, step):
        return step > 1 or far_way(m) == way

    for step in range(1, HOPS + 1):
        for m in range(3):
            if step == 1:
                a, b = pairs[m]
                own[m] = dot_tn(a[:, mine], b[...])
                arrived(sib_recv.at[m], sib_rs.at[m])
                own[m] = own[m] + sib_recv[m].astype(F32)
            for way in range(2):
                if not goes(m, way, step):
                    continue
                dist = HOPS + 1 - step
                part = own[m, shard(dist if way == 0 else -dist), :]
                if step > 1 and goes(m, way, step - 1):
                    arrived(rs_recv.at[m, way, step - 2], rs_rs.at[m, way, step - 2])
                    part = part + rs_recv[m, way, step - 2].astype(F32)
                rs_send[m, way, step - 1] = part.astype(BF16)
                send(
                    rs_send.at[m, way, step - 1], rs_recv.at[m, way, step - 1],
                    rs_ss.at[m, way, step - 1], rs_rs.at[m, way, step - 1], zway[way],
                )
        push(1)
        if step > 1:
            pass_values(1)
        own_tile(step - 1)

    for m in range(3):
        part = own[m, shard(0), :]
        for way in range(2):
            arrived(rs_recv.at[m, way, HOPS - 1], rs_rs.at[m, way, HOPS - 1])
            part = part + rs_recv[m, way, HOPS - 1].astype(F32)
        x_send[m] = part.astype(BF16)
        send(x_send.at[m], x_recv.at[m], x_ss.at[m], x_rs.at[m], xhp)
    push(2)
    pass_values(2)

    def rows_of(d, cc):
        return pl.ds(pl.multiple_of(cc * HALF + ((z + NZ + d) % NZ) * SHARD, SHARD), SHARD)

    def to_ring(m, d, way, dist):
        r = gfull.at[m, rows_of(d, core)]
        send(r, r, ag_ss.at[m, way, dist - 1], ag_rs.at[m, way, dist - 1], zway[way])

    def to_core(m, d):
        r = gfull.at[m, rows_of(d, core)]
        i = d % NZ
        send(r, r, sg_ss.at[m, i], sg_rs.at[m, i], sib)

    for m in range(3):
        arrived(x_recv.at[m], x_rs.at[m])
        both = x_send[m].astype(F32) + x_recv[m].astype(F32)
        gfull[m, rows_of(0, core), :] = both.astype(BF16)
        to_ring(m, 0, 0, 1)
        to_ring(m, 0, 1, 1)
        to_core(m, 0)

    for dist in range(1, HOPS + 1):
        for m in range(3):
            for way in range(2):
                if dist == HOPS and far_way(m) != way:
                    continue
                d = -dist if way == 0 else dist
                arrived(gfull.at[m, rows_of(d, core)], ag_rs.at[m, way, dist - 1])
                if dist + 1 < HOPS or (dist + 1 == HOPS and far_way(m) == way):
                    to_ring(m, d, way, dist + 1)
                to_core(m, d)
        if dist == 1:
            push(1)
        if dist < HOPS:
            pass_values(1)
        if dist == 1:
            w_on(0)
        if dist == HOPS - 1:
            w_swap()
            pulled(0, 8)
            halo_tile(2)
            halo_tile(3)

    w_on(1)
    pulled(8, len(pieces))
    for t in range(NT // 2):
        halo_tile(t)

    squares = jnp.zeros((1, HD), F32)
    for m in range(3):
        for d in range(NZ):
            arrived(gfull.at[m, rows_of(d, 1 - core)], sg_rs.at[m, d])
        g = gfull[m].astype(F32)
        squares = squares + jnp.sum(g * g, axis=0, keepdims=True)

    gnorm = jnp.sqrt(jnp.sum(squares, axis=1, keepdims=True) + EPS)
    factor = jnp.minimum(1.0, GRAD_LIMIT / gnorm)
    for m, (old, new) in enumerate(((w2, n2), (w1, n1), (w3, n3))):
        w = old[0].astype(F32)
        u = w - factor * gfull[m].astype(F32)
        before = jnp.sqrt(jnp.sum(w * w, axis=0, keepdims=True) + EPS)
        after = jnp.sqrt(jnp.sum(u * u, axis=0, keepdims=True) + EPS)
        new[...] = (u * (before / after)).astype(BF16)

    h_own = head
    h_mate = xl * 4 + y_mate
    h_pair = xl * 4 + y_pair
    h_far = xl * 4 + y_far
    x_own = (1 - xl) * 4 + y
    x_mate = (1 - xl) * 4 + y_mate
    x_pair = (1 - xl) * 4 + y_pair
    x_far = (1 - xl) * 4 + y_far

    def readout(half, i):
        r = pl.ds(pl.multiple_of(half * MY + i * TT, TT), TT)
        qt = q[r, :]
        g = dot(qt, n1[...])
        u = dot(qt, n3[...])
        a = (g * sigmoid(g) * u).astype(BF16)
        f = dot(a, n2[...])
        ms = jnp.mean(f * f, axis=1, keepdims=True)
        nrm = f * lax.rsqrt(ms + EPS) * gain[...]
        return (nrm + acc[r, :]).astype(BF16)

    def slot(h, t):
        return gat.at[h, pl.ds(t * GT, GT)]

    def got(h, t):
        arrived(slot(h, t), g_rs.at[t, h])

    def pass_on(h, t, kind, dev):
        send(slot(h, t), slot(h, t), g_ss.at[t, kind], g_rs.at[t, h], dev)

    def own_out(t):
        pass_on(h_own, t, 0, xp)
        pass_on(h_own, t, 1, mate)

    def other_out(t):
        send(oth.at[pl.ds(t * GT, GT)], slot(h_own, t), g_ss.at[t, 2], g_rs.at[t, h_own], pair)

    def near_one(t):
        if t % 2 == 0:
            got(x_own, t)
            pass_on(x_own, t, 3, mate)
        else:
            got(h_mate, t)
            pass_on(h_mate, t, 3, xp)

    def near_rest(t):
        got(h_mate if t % 2 == 0 else x_own, t)
        got(x_mate, t)

    def pair_one(t):
        got(h_pair, t)
        pass_on(h_pair, t, 4, mate)
        pass_on(h_pair, t, 5, xp)

    def pair_two(t):
        if t % 2 == 0:
            got(h_far, t)
            pass_on(h_far, t, 6, xp)
        else:
            got(x_pair, t)
            pass_on(x_pair, t, 6, mate)

    def pair_rest(t):
        got(x_pair if t % 2 == 0 else h_far, t)
        got(x_far, t)

    def place(i):
        return pl.ds(i * PT, PT), pl.ds(pl.multiple_of(group * MY + i * PT, PT), PT)

    def all_heads(r, w):
        o = dot(gat[0, r, :], w[pl.ds(0, HD), :])
        for h in range(1, HEADS):
            o = o + dot(gat[h, r, :], w[pl.ds(h * HD, HD), :])
        return o.astype(BF16)

    def out_part(half, j):
        lo, n = OUT_PARTS[j]
        return pl.ds(pl.multiple_of(half * MY + lo, GT), n)

    def project_pair(j):
        lo, n = OUT_PARTS[j]
        r = pl.ds(lo, n)
        opair[r, :] = all_heads(r, wo2)
        send(opair.at[r], outv.at[out_part(group, j)], o_ss.at[j], o_rs.at[j], pair)

    def project(i):
        r, here = place(i)
        outv[here, :] = all_heads(r, wo)
        pltpu.make_async_copy(outv.at[here], out_ref.at[here], out_sem.at[0, i]).start()

    for i in range(MY // TT):
        r = pl.ds(i * TT, TT)
        gat[h_own, r, :] = readout(group, i)
        for t in range(i * TT // GT, (i + 1) * TT // GT):
            own_out(t)
        oth[r, :] = readout(1 - group, i)
        for t in range(i * TT // GT, (i + 1) * TT // GT):
            other_out(t)
    loads[10].wait()
    PER = PT // GT
    for step in range(NG + 5):
        if step < NG:
            near_one(step)
        if 0 <= step - ONE_LAG < NG:
            pair_one(step - ONE_LAG)
        if step == 1:
            w_on(2)
        if step == 2:
            w_on(3)
            w_on(4)
        if 0 <= step - TWO_LAG < NG:
            pair_two(step - TWO_LAG)
        p = step - 4
        if 0 <= p < NG:
            near_rest(p)
            pair_rest(p)
            if p == PER - 1:
                for j in range(WP + 1):
                    arrived(w_part(1 - core, j), ws_rs.at[j])
            if (p + 1) % PER == 0:
                i = p // PER
                if i < NP - 1:
                    project_pair(i)
                if i < NP - 2:
                    project(i)
            if p == NG - 2:
                project_pair(NP - 1)
            if p == NG - 1:
                project_pair(NP)
    project(NP - 2)
    project(NP - 1)

    for j in range(NP + 1):
        there = out_part(1 - group, j)
        arrived(outv.at[there], o_rs.at[j])
        pltpu.make_async_copy(outv.at[there], out_ref.at[there], out_sem.at[1, j]).start()
    for i in range(NP):
        r = place(i)[1]
        pltpu.make_async_copy(outv.at[r], out_ref.at[r], out_sem.at[0, i]).wait()
    for j in range(NP + 1):
        r = out_part(1 - group, j)
        pltpu.make_async_copy(outv.at[r], out_ref.at[r], out_sem.at[1, j]).wait()
    for c in sends:
        c.wait_send()

    @pl.when(relays)
    def _():
        for c in passed:
            c.wait_send()


def hand_over(src, dst):
    dst[...] = src[...]


def per_device(*args):
    any_spec = pl.BlockSpec(memory_space=pl.ANY)
    in_specs = [any_spec] * 10
    in_specs[4] = pl.BlockSpec(memory_space=pltpu.SMEM)
    V = pltpu.VMEM
    D = pltpu.SemaphoreType.DMA
    scratch = [
        V((TOK, HD), BF16), V((TOK, HD), BF16), V((TOK, HD), BF16),
        V((HALO, HD), BF16), V((HALO, HD), BF16), V((HALO, HD), BF16),
        V((1, HD, HD), BF16), V((1, HD, HD), BF16), V((1, HD, HD), BF16),
        V((HEADS * HD, COLS), BF16), V((1, TOK), F32), V((1, HD), F32),
        V((TOK, HD), BF16), V((TOK, HD), BF16), V((TOK, HD), BF16), V((TOK, HD), BF16),
        V((3, HALF, HD), BF16), V((3, HALF, HD), BF16), V((3, HALF, HD), F32),
        V((3, 2, HOPS, SHARD, HD), BF16), V((3, 2, HOPS, SHARD, HD), BF16),
        V((3, SHARD, HD), BF16), V((3, SHARD, HD), BF16), V((3, HD, HD), BF16),
        V((HD, HD), BF16), V((HD, HD), BF16), V((HD, HD), BF16),
        V((TOK, 1), F32), V((TOK, 1), F32), V((TOK, HD), F32),
        V((HEADS, MY, HD), BF16), V((MY, HD), BF16),
        V((HEADS * HD, COLS), BF16),
        V((MY, COLS), BF16), V((TOK, COLS), BF16),
        D((11,)), D((2, NP + 1)), D((16,)), D((16,)), D((16,)), D((16,)), D((3,)), D((3,)),
        D((3, 2, HOPS)), D((3, 2, HOPS)), D((3,)), D((3,)),
        D((3, 2, HOPS)), D((3, 2, HOPS)), D((3, NZ)), D((3, NZ)),
        D((NG, 7)), D((NG, HEADS)), D((WP + 1,)), D((WP + 1,)), D((WP + 1,)), D((WP + 1,)), D((NP + 1,)), D((NP + 1,)),
    ]
    out = pl.pallas_call(
        body,
        out_shape=jax.ShapeDtypeStruct((TOK, COLS), BF16),
        in_specs=in_specs,
        out_specs=any_spec,
        scratch_shapes=scratch,
        compiler_params=pltpu.CompilerParams(
            collective_id=0, has_side_effects=True, vmem_limit_bytes=60 << 20
        ),
        cost_estimate=pl.CostEstimate(flops=13_400_000_000, bytes_accessed=15_000_000, transcendentals=3_000_000),
        name="ttt_layer",
    )(*args)
    return pl.pallas_call(
        hand_over,
        out_shape=jax.ShapeDtypeStruct((TOK, COLS), BF16),
        grid=(2,),
        in_specs=[pl.BlockSpec((TOK // 2, COLS), lambda i: (i, 0))],
        out_specs=pl.BlockSpec((TOK // 2, COLS), lambda i: (i, 0)),
        cost_estimate=pl.CostEstimate(flops=0, bytes_accessed=4 * TOK * COLS, transcendentals=0),
        name="hand_over",
    )(out)


def solution(mesh):
    placed = (
        P("ctx", "head"),
        P("ctx", "head"),
        P("ctx", "head"),
        P("head", "ctx"),
        P("head", "ctx"),
        P("head", None, None),
        P("head", None, None),
        P("head", None, None),
        P("head", None),
        P(None, "head"),
    )
    return jax.shard_map(
        per_device, mesh=mesh, in_specs=placed, out_specs=P("ctx", "head"), check_vma=False
    )
```

```python
import jax
import jax.numpy as jnp
from jax import lax
from jax.sharding import PartitionSpec as P
from jax.experimental import pallas as pl
from jax.experimental.pallas import tpu as pltpu

MESH = pl.DeviceIdType.MESH
F32 = jnp.float32
BF16 = jnp.bfloat16

TOK = 1024
HD = 512
BL = 512
HALO = 1024
NZ = 8
NY = 4
HEADS = 8
COLS = 640
HALF = 256
SHARD = 32
HOPS = NZ // 2
TT = 256
NT = TOK // TT
MY = TOK // 2
GT = 64
NG = MY // GT
PT = 128
NP = MY // PT
OUT_PARTS = ((0, 128), (128, 128), (256, 128), (384, 64), (448, 64))
WP = HEADS // 2
ONE_LAG = 0
TWO_LAG = 3
REST_LAG = 6
HP = 128
GRAD_LIMIT = 24.0
EPS = 1e-6
MASKED = -1e30


def sigmoid(x):
    return 0.5 * jnp.tanh(0.5 * x) + 0.5


def dot(a, b):
    return jnp.dot(a, b, preferred_element_type=F32)


def dot_nt(a, b):
    return lax.dot_general(a, b, (((1,), (1,)), ((), ())), preferred_element_type=F32)


def dot_tn(a, b):
    return lax.dot_general(a, b, (((0,), (0,)), ((), ())), preferred_element_type=F32)


def far_way(m):
    return m % 2


def body(
    q_ref, k_ref, v_ref, rate_ref, win_ref, w1_ref, w3_ref, w2_ref, gain_ref, wo_ref,
    out_ref,
    q, k, v, hk, hv, stage, w1, w3, w2, wo, rate, gain,
    hid, tgt, bg, bu,
    sib_send, sib_recv, own, rs_send, rs_recv, x_send, x_recv, gfull,
    n1, n3, n2, m_run, l_run, acc, gat, oth, wo2, opair, outv,
    load_sem, out_sem, halo_ss, halo_rs, stage_ss, stage_rs, sib_ss, sib_rs, rs_ss, rs_rs, x_ss, x_rs,
    ag_ss, ag_rs, sg_ss, sg_rs, g_ss, g_rs, w_ss, w_rs, ws_ss, ws_rs, o_ss, o_rs,
):
    ctx = lax.axis_index("ctx")
    head = lax.axis_index("head")
    z = ctx // 4
    xh = (ctx // 2) % 2
    core = ctx % 2
    xl = head // 4
    y = head % 4

    def at_ctx(zz, xx, cc):
        return (zz * 4 + xx * 2 + cc, head)

    def at_head(xx, yy):
        return (ctx, xx * 4 + yy)

    sib = at_ctx(z, xh, 1 - core)
    xhp = at_ctx(z, 1 - xh, core)
    zway = (at_ctx((z + 1) % NZ, xh, core), at_ctx((z + NZ - 1) % NZ, xh, core))
    nxt = ((ctx + 1) % 32, head)
    prv = ((ctx + 31) % 32, head)
    over = at_ctx((z + 1) % NZ, xh, 1 - core)
    under = at_ctx((z + NZ - 1) % NZ, xh, 1 - core)
    crosses = jnp.logical_and(core == 1, xh == 1)
    relays = jnp.logical_and(core == 1, xh == 0)
    xp = at_head(1 - xl, y)
    group = y // 2
    y_pair = 3 - y
    y_mate = 1 - y + 4 * group
    y_far = 3 - y_mate
    pair = at_head(xl, y_pair)
    mate = at_head(xl, y_mate)

    bar = pltpu.get_barrier_semaphore()
    partners = [sib, xhp, zway[0], zway[1], xp, pair, mate, prv, under]
    for p in partners:
        pl.semaphore_signal(bar, inc=1, device_id=p, device_id_type=MESH)

    loads = []
    lo, hi = pl.ds(0, TOK // 2), pl.ds(TOK // 2, TOK // 2)
    for i, (src, dst) in enumerate(
        ((k_ref.at[lo], k.at[lo]), (w1_ref, w1), (w3_ref, w3), (rate_ref, rate),
         (v_ref.at[lo], v.at[lo]), (w2_ref, w2), (k_ref.at[hi], k.at[hi]), (v_ref.at[hi], v.at[hi]),
         (q_ref, q), (gain_ref, gain), (wo_ref, wo))
    ):
        c = pltpu.make_async_copy(src, dst, load_sem.at[i])
        if i < 8:
            c.start()
        loads.append(c)

    sends = []

    def copy(src, dst, ss, rs, dev):
        return pltpu.make_async_remote_copy(
            src_ref=src, dst_ref=dst, send_sem=ss, recv_sem=rs, device_id=dev, device_id_type=MESH
        )

    def send(src, dst, ss, rs, dev):
        c = copy(src, dst, ss, rs, dev)
        c.start()
        sends.append(c)
        return c

    def arrived(dst, rs):
        pltpu.make_async_remote_copy(
            src_ref=dst, dst_ref=dst, send_sem=rs, recv_sem=rs, device_id=sib, device_id_type=MESH
        ).wait_recv()

    pieces = [
        (src, dst, blk * BL + i * HP)
        for blk in (1, 0)
        for i in range(BL // HP)
        for src, dst in ((v_ref, hv), (k_ref, hk))
    ]
    pushed = []
    passed = []

    def push(count):
        for _ in range(count):
            i = len(pushed)
            src, dst, lo = pieces[i]
            pushed.append(i)
            r = pl.ds(lo, HP)
            if dst is hk:
                send(src.at[r], dst.at[r], halo_ss.at[i], halo_rs.at[i], nxt)
                continue

            c = copy(src.at[r], dst.at[r], halo_ss.at[i], halo_rs.at[i], nxt)
            first_leg = copy(src.at[r], stage.at[r], halo_ss.at[i], stage_rs.at[i], xhp)
            sends.append(c)

            @pl.when(jnp.logical_not(crosses))
            def _():
                c.start()

            @pl.when(crosses)
            def _():
                first_leg.start()

    def pass_values(count):
        for _ in range(count):
            i = 2 * len(passed)
            src, dst, lo = pieces[i]
            r = pl.ds(lo, HP)
            c = copy(stage.at[r], dst.at[r], stage_ss.at[i], halo_rs.at[i], over)
            passed.append(c)

            @pl.when(relays)
            def _():
                arrived(stage.at[r], stage_rs.at[i])
                c.start()

    def pulled(lo, hi):
        for i in range(lo, hi):
            src, dst, row = pieces[i]
            arrived(dst.at[pl.ds(row, HP)], halo_rs.at[i])

    for c in loads[:6]:
        c.wait()

    def grad_tile(t, carry):
        r = pl.ds(pl.multiple_of(t * TT, TT), TT)
        kt = k[r, :]
        gp = dot(kt, w1[0])
        up = dot(kt, w3[0])
        s = sigmoid(gp)
        sv = gp * s
        hid[r, :] = (sv * up).astype(BF16)
        row = rate[:, r]
        eye = lax.broadcasted_iota(jnp.int32, (TT, TT), 0) == lax.broadcasted_iota(
            jnp.int32, (TT, TT), 1
        )
        col = jnp.sum(jnp.where(eye, row, 0.0), axis=1, keepdims=True)
        tg = (-col * v[r, :].astype(F32)).astype(BF16)
        tgt[r, :] = tg
        ba = dot_nt(tg, w2[0])
        bg[r, :] = (ba * up * (s * (1.0 + gp * (1.0 - s)))).astype(BF16)
        bu[r, :] = (ba * sv).astype(BF16)
        return carry

    lax.fori_loop(0, 2, grad_tile, 0)
    pl.semaphore_wait(bar, len(partners))
    push(6)

    keep = 2 + z % 2
    lack = 3 - z % 2
    half_rows = HD // 2

    def w_at(cc, i, lo=0, n=HD):
        return wo2.at[pl.ds(pl.multiple_of((cc * WP + i) * HD + lo, half_rows), n)]

    def w_part(cc, j):
        return (
            w_at(cc, keep), w_at(cc, 0), w_at(cc, 1),
            w_at(cc, lack, 0, half_rows), w_at(cc, lack, half_rows, half_rows),
        )[j]

    for j, i in enumerate((keep, 0, 1)):
        r = pl.ds(pl.multiple_of((core * WP + i) * HD, HD), HD)
        send(wo_ref.at[r], wo2.at[r], w_ss.at[j], w_rs.at[j], pair)

    def w_swap():
        for way in range(2):
            r = w_at(core, keep, way * half_rows, half_rows)
            send(r, r, w_ss.at[3 + way], w_rs.at[3 + way], zway[way])

    for c in loads[6:8]:
        c.wait()
    for c in loads[8:]:
        c.start()
    lax.fori_loop(2, NT, grad_tile, 0)
    push(3)

    def w_on(j):
        r = w_part(core, j)
        arrived(r, w_rs.at[j])
        send(r, r, ws_ss.at[j], ws_rs.at[j], sib)

    theirs = pl.ds(pl.multiple_of((1 - core) * HALF, HALF), HALF)
    mine = pl.ds(pl.multiple_of(core * HALF, HALF), HALF)
    pairs = ((hid, tgt), (k, bg), (k, bu))
    for m, (a, b) in enumerate(pairs):
        sib_send[m] = dot_tn(a[:, theirs], b[...]).astype(BF16)
        send(sib_send.at[m], sib_recv.at[m], sib_ss.at[m], sib_rs.at[m], sib)

    for c in loads[8:10]:
        c.wait()
    scale = HD ** -0.5
    reach = [win_ref[0, 0], win_ref[0, 1]]

    def own_tile(t):
        r = pl.ds(t * TT, TT)
        blk = t // 2
        width = (t + 1) * TT
        s = dot_nt(q[r, :], k[pl.ds(0, width), :]) * scale
        qpos = lax.broadcasted_iota(jnp.int32, (TT, width), 0) + t * TT
        kpos = lax.broadcasted_iota(jnp.int32, (TT, width), 1)
        s = jnp.where(kpos <= qpos, s, MASKED)
        if blk == 1:
            far = jnp.where(reach[1] >= 1, 0.0, MASKED)
            s = s + jnp.where(kpos < BL, far, 0.0)
        top = jnp.max(s, axis=1, keepdims=True)
        p = jnp.exp(s - top)
        m_run[r, :] = top
        l_run[r, :] = jnp.sum(p, axis=1, keepdims=True)
        acc[r, :] = dot(p.astype(BF16), v[pl.ds(0, width), :])

    first = ctx == 0

    def halo_tile(t):
        r = pl.ds(t * TT, TT)
        blk = t // 2
        if blk == 0:
            lo, width = 0, HALO
        else:
            lo, width = BL, BL
        s = dot_nt(q[r, :], hk[pl.ds(lo, width), :]) * scale
        near = jnp.where(jnp.logical_or(reach[blk] < (1 if blk == 0 else 2), first), MASKED, 0.0)
        if blk == 0:
            far = jnp.where(jnp.logical_or(reach[blk] < 2, first), MASKED, 0.0)
            kpos = lax.broadcasted_iota(jnp.int32, (TT, width), 1)
            s = s + jnp.where(kpos < BL, far, near)
        else:
            s = s + near
        old = m_run[r, :]
        top = jnp.maximum(old, jnp.max(s, axis=1, keepdims=True))
        p = jnp.exp(s - top)
        keep = jnp.exp(old - top)
        total = l_run[r, :] * keep + jnp.sum(p, axis=1, keepdims=True)
        o = acc[r, :] * keep + dot(p.astype(BF16), hv[pl.ds(lo, width), :])
        acc[r, :] = o / total

    def shard(d):
        return pl.ds(pl.multiple_of(((z + NZ + d) % NZ) * SHARD, SHARD), SHARD)

    def goes(m, way, step):
        return step > 1 or far_way(m) == way

    for step in range(1, HOPS + 1):
        for m in range(3):
            if step == 1:
                a, b = pairs[m]
                own[m] = dot_tn(a[:, mine], b[...])
                arrived(sib_recv.at[m], sib_rs.at[m])
                own[m] = own[m] + sib_recv[m].astype(F32)
            for way in range(2):
                if not goes(m, way, step):
                    continue
                dist = HOPS + 1 - step
                part = own[m, shard(dist if way == 0 else -dist), :]
                if step > 1 and goes(m, way, step - 1):
                    arrived(rs_recv.at[m, way, step - 2], rs_rs.at[m, way, step - 2])
                    part = part + rs_recv[m, way, step - 2].astype(F32)
                rs_send[m, way, step - 1] = part.astype(BF16)
                send(
                    rs_send.at[m, way, step - 1], rs_recv.at[m, way, step - 1],
                    rs_ss.at[m, way, step - 1], rs_rs.at[m, way, step - 1], zway[way],
                )
        push(1)
        if step > 1:
            pass_values(1)
        own_tile(step - 1)

    for m in range(3):
        part = own[m, shard(0), :]
        for way in range(2):
            arrived(rs_recv.at[m, way, HOPS - 1], rs_rs.at[m, way, HOPS - 1])
            part = part + rs_recv[m, way, HOPS - 1].astype(F32)
        x_send[m] = part.astype(BF16)
        send(x_send.at[m], x_recv.at[m], x_ss.at[m], x_rs.at[m], xhp)
    push(2)
    pass_values(2)

    def rows_of(d, cc):
        return pl.ds(pl.multiple_of(cc * HALF + ((z + NZ + d) % NZ) * SHARD, SHARD), SHARD)

    def to_ring(m, d, way, dist):
        r = gfull.at[m, rows_of(d, core)]
        send(r, r, ag_ss.at[m, way, dist - 1], ag_rs.at[m, way, dist - 1], zway[way])

    def to_core(m, d):
        r = gfull.at[m, rows_of(d, core)]
        i = d % NZ
        send(r, r, sg_ss.at[m, i], sg_rs.at[m, i], sib)

    for m in range(3):
        arrived(x_recv.at[m], x_rs.at[m])
        both = x_send[m].astype(F32) + x_recv[m].astype(F32)
        gfull[m, rows_of(0, core), :] = both.astype(BF16)
        to_ring(m, 0, 0, 1)
        to_ring(m, 0, 1, 1)
        to_core(m, 0)

    for dist in range(1, HOPS + 1):
        for m in range(3):
            for way in range(2):
                if dist == HOPS and far_way(m) != way:
                    continue
                d = -dist if way == 0 else dist
                arrived(gfull.at[m, rows_of(d, core)], ag_rs.at[m, way, dist - 1])
                if dist + 1 < HOPS or (dist + 1 == HOPS and far_way(m) == way):
                    to_ring(m, d, way, dist + 1)
                to_core(m, d)
        if dist == 1:
            push(1)
        if dist < HOPS:
            pass_values(1)
        if dist == 1:
            w_on(0)
        if dist == HOPS - 1:
            w_swap()
            pulled(0, 8)
            halo_tile(2)
            halo_tile(3)

    w_on(1)
    pulled(8, len(pieces))
    for t in range(NT // 2):
        halo_tile(t)

    squares = jnp.zeros((1, HD), F32)
    for m in range(3):
        for d in range(NZ):
            arrived(gfull.at[m, rows_of(d, 1 - core)], sg_rs.at[m, d])
        g = gfull[m].astype(F32)
        squares = squares + jnp.sum(g * g, axis=0, keepdims=True)

    gnorm = jnp.sqrt(jnp.sum(squares, axis=1, keepdims=True) + EPS)
    factor = jnp.minimum(1.0, GRAD_LIMIT / gnorm)
    for m, (old, new) in enumerate(((w2, n2), (w1, n1), (w3, n3))):
        w = old[0].astype(F32)
        u = w - factor * gfull[m].astype(F32)
        before = jnp.sqrt(jnp.sum(w * w, axis=0, keepdims=True) + EPS)
        after = jnp.sqrt(jnp.sum(u * u, axis=0, keepdims=True) + EPS)
        new[...] = (u * (before / after)).astype(BF16)

    h_own = head
    h_mate = xl * 4 + y_mate
    h_pair = xl * 4 + y_pair
    h_far = xl * 4 + y_far
    x_own = (1 - xl) * 4 + y
    x_mate = (1 - xl) * 4 + y_mate
    x_pair = (1 - xl) * 4 + y_pair
    x_far = (1 - xl) * 4 + y_far

    def readout(half, i):
        r = pl.ds(pl.multiple_of(half * MY + i * TT, TT), TT)
        qt = q[r, :]
        g = dot(qt, n1[...])
        u = dot(qt, n3[...])
        a = (g * sigmoid(g) * u).astype(BF16)
        f = dot(a, n2[...])
        ms = jnp.mean(f * f, axis=1, keepdims=True)
        nrm = f * lax.rsqrt(ms + EPS) * gain[...]
        return (nrm + acc[r, :]).astype(BF16)

    def slot(h, t):
        return gat.at[h, pl.ds(t * GT, GT)]

    def got(h, t):
        arrived(slot(h, t), g_rs.at[t, h])

    def pass_on(h, t, kind, dev):
        send(slot(h, t), slot(h, t), g_ss.at[t, kind], g_rs.at[t, h], dev)

    def own_out(t):
        pass_on(h_own, t, 0, xp)
        pass_on(h_own, t, 1, mate)

    def other_out(t):
        send(oth.at[pl.ds(t * GT, GT)], slot(h_own, t), g_ss.at[t, 2], g_rs.at[t, h_own], pair)

    def near_one(t):
        if t % 2 == 0:
            got(x_own, t)
            pass_on(x_own, t, 3, mate)
        else:
            got(h_mate, t)
            pass_on(h_mate, t, 3, xp)

    def near_rest(t):
        got(h_mate if t % 2 == 0 else x_own, t)
        got(x_mate, t)

    def pair_one(t):
        got(h_pair, t)
        pass_on(h_pair, t, 4, mate)
        pass_on(h_pair, t, 5, xp)

    def pair_two(t):
        if t % 2 == 0:
            got(h_far, t)
            pass_on(h_far, t, 6, xp)
        else:
            got(x_pair, t)
            pass_on(x_pair, t, 6, mate)

    def pair_rest(t):
        got(x_pair if t % 2 == 0 else h_far, t)
        got(x_far, t)

    def place(i):
        return pl.ds(i * PT, PT), pl.ds(pl.multiple_of(group * MY + i * PT, PT), PT)

    def all_heads(r, w):
        o = dot(gat[0, r, :], w[pl.ds(0, HD), :])
        for h in range(1, HEADS):
            o = o + dot(gat[h, r, :], w[pl.ds(h * HD, HD), :])
        return o.astype(BF16)

    def out_part(half, j):
        lo, n = OUT_PARTS[j]
        return pl.ds(pl.multiple_of(half * MY + lo, GT), n)

    def project_pair(j):
        lo, n = OUT_PARTS[j]
        r = pl.ds(lo, n)
        opair[r, :] = all_heads(r, wo2)
        send(opair.at[r], outv.at[out_part(group, j)], o_ss.at[j], o_rs.at[j], pair)

    def project(i):
        r, here = place(i)
        outv[here, :] = all_heads(r, wo)
        pltpu.make_async_copy(outv.at[here], out_ref.at[here], out_sem.at[0, i]).start()

    for i in range(MY // TT):
        r = pl.ds(i * TT, TT)
        gat[h_own, r, :] = readout(group, i)
        for t in range(i * TT // GT, (i + 1) * TT // GT):
            own_out(t)
        oth[r, :] = readout(1 - group, i)
        for t in range(i * TT // GT, (i + 1) * TT // GT):
            other_out(t)
    loads[10].wait()
    PER = PT // GT
    for step in range(NG + REST_LAG):
        if step < NG:
            near_one(step)
        if 0 <= step - ONE_LAG < NG:
            pair_one(step - ONE_LAG)
        if step == 1:
            w_on(2)
        if step == 2:
            w_on(3)
            w_on(4)
        if 0 <= step - TWO_LAG < NG:
            pair_two(step - TWO_LAG)
        p = step - REST_LAG
        if 0 <= p < NG:
            near_rest(p)
            pair_rest(p)
            if p == PER - 1:
                for j in range(WP + 1):
                    arrived(w_part(1 - core, j), ws_rs.at[j])
            if (p + 1) % PER == 0:
                i = p // PER
                if i < NP - 1:
                    project_pair(i)
                if i < NP - 2:
                    project(i)
            if p == NG - 2:
                project_pair(NP - 1)
            if p == NG - 1:
                project_pair(NP)
    project(NP - 2)
    project(NP - 1)

    for j in range(NP + 1):
        there = out_part(1 - group, j)
        arrived(outv.at[there], o_rs.at[j])
        pltpu.make_async_copy(outv.at[there], out_ref.at[there], out_sem.at[1, j]).start()
    for i in range(NP):
        r = place(i)[1]
        pltpu.make_async_copy(outv.at[r], out_ref.at[r], out_sem.at[0, i]).wait()
    for j in range(NP + 1):
        r = out_part(1 - group, j)
        pltpu.make_async_copy(outv.at[r], out_ref.at[r], out_sem.at[1, j]).wait()
    for c in sends:
        c.wait_send()

    @pl.when(relays)
    def _():
        for c in passed:
            c.wait_send()


def hand_over(src, dst):
    dst[...] = src[...]


def per_device(*args):
    any_spec = pl.BlockSpec(memory_space=pl.ANY)
    in_specs = [any_spec] * 10
    in_specs[4] = pl.BlockSpec(memory_space=pltpu.SMEM)
    V = pltpu.VMEM
    D = pltpu.SemaphoreType.DMA
    scratch = [
        V((TOK, HD), BF16), V((TOK, HD), BF16), V((TOK, HD), BF16),
        V((HALO, HD), BF16), V((HALO, HD), BF16), V((HALO, HD), BF16),
        V((1, HD, HD), BF16), V((1, HD, HD), BF16), V((1, HD, HD), BF16),
        V((HEADS * HD, COLS), BF16), V((1, TOK), F32), V((1, HD), F32),
        V((TOK, HD), BF16), V((TOK, HD), BF16), V((TOK, HD), BF16), V((TOK, HD), BF16),
        V((3, HALF, HD), BF16), V((3, HALF, HD), BF16), V((3, HALF, HD), F32),
        V((3, 2, HOPS, SHARD, HD), BF16), V((3, 2, HOPS, SHARD, HD), BF16),
        V((3, SHARD, HD), BF16), V((3, SHARD, HD), BF16), V((3, HD, HD), BF16),
        V((HD, HD), BF16), V((HD, HD), BF16), V((HD, HD), BF16),
        V((TOK, 1), F32), V((TOK, 1), F32), V((TOK, HD), F32),
        V((HEADS, MY, HD), BF16), V((MY, HD), BF16),
        V((HEADS * HD, COLS), BF16),
        V((MY, COLS), BF16), V((TOK, COLS), BF16),
        D((11,)), D((2, NP + 1)), D((16,)), D((16,)), D((16,)), D((16,)), D((3,)), D((3,)),
        D((3, 2, HOPS)), D((3, 2, HOPS)), D((3,)), D((3,)),
        D((3, 2, HOPS)), D((3, 2, HOPS)), D((3, NZ)), D((3, NZ)),
        D((NG, 7)), D((NG, HEADS)), D((WP + 1,)), D((WP + 1,)), D((WP + 1,)), D((WP + 1,)), D((NP + 1,)), D((NP + 1,)),
    ]
    out = pl.pallas_call(
        body,
        out_shape=jax.ShapeDtypeStruct((TOK, COLS), BF16),
        in_specs=in_specs,
        out_specs=any_spec,
        scratch_shapes=scratch,
        compiler_params=pltpu.CompilerParams(
            collective_id=0, has_side_effects=True, vmem_limit_bytes=60 << 20
        ),
        cost_estimate=pl.CostEstimate(flops=13_400_000_000, bytes_accessed=15_000_000, transcendentals=3_000_000),
        name="ttt_layer",
    )(*args)
    return pl.pallas_call(
        hand_over,
        out_shape=jax.ShapeDtypeStruct((TOK, COLS), BF16),
        grid=(4,),
        in_specs=[pl.BlockSpec((TT, COLS), lambda i: (i, 0))],
        out_specs=pl.BlockSpec((TT, COLS), lambda i: (i, 0)),
        cost_estimate=pl.CostEstimate(flops=0, bytes_accessed=4 * TOK * COLS, transcendentals=0),
        name="hand_over",
    )(out)


def solution(mesh):
    placed = (
        P("ctx", "head"),
        P("ctx", "head"),
        P("ctx", "head"),
        P("head", "ctx"),
        P("head", "ctx"),
        P("head", None, None),
        P("head", None, None),
        P("head", None, None),
        P("head", None),
        P(None, "head"),
    )
    return jax.shard_map(
        per_device, mesh=mesh, in_specs=placed, out_specs=P("ctx", "head"), check_vma=False
    )
```
